32 devices in a mesh: district: 8 (over z, y), blk: 4 (over x, core).
Axes of the slice: x: 2, y: 2, z: 4, core: 2. Of those that a mesh axis runs over, the one named last changes fastest.
Arguments:
- view_factor: bfloat16 [192, 24, 128, 128], P(('district', 'blk')), may hold values from 0 to 0.00064849854
- view_cols: int32 [192, 24], P(('district', 'blk')), may hold values from 0 to 47, as said below
- border_list: int32 [96], P(('district', 'blk')), may hold values from 0 to 5, as said below
- radiosity: bfloat16 [16, 24576], P(None, ('district', 'blk')), may hold values from 0.05 to 7.5, as said below
- reflectance: bfloat16 [16, 24576], P(None, ('district', 'blk')), may hold values from 0.29882812 to 0.8984375
- emissivity: float32 [24576], P(('district', 'blk')), may hold values from 0.6 to 0.98
- band_weight: float32 [16], replicated, may hold values from 0.1 to 0.6
- surface_temp: float32 [24576], P(('district', 'blk')), may hold values from 0.8 to 1.3
- patch_cell: int32 [24576], P(('district', 'blk')), may hold values from 0 to 16383
- air: float32 [64, 128, 4096], P(None, 'district', 'blk'), may hold values from -6 to 6
Outputs:
- radiosity_next: float32 [16, 24576], P(None, ('district', 'blk'))
- surface_next: float32 [24576], P(('district', 'blk'))
- air_next: float32 [64, 128, 4096], P(None, 'district', 'blk')
The draws below stay inside these ranges and needn't reach their ends.
Inputs may be any that keep to these rules, and one draw needn't show every extreme that they name: `view_cols`: within one block row the 24 column numbers are different. `border_list`: the 3 entries of one device are different local block numbers. `radiosity`: Positive; values vary strongly from block to block.
All inputs are finite; a program needn't handle non-finite values.
Results may differ from the reference program's by a relative error of at most 0.0003.
Values may be sent and summed in bfloat16 or wider, within the bound.
No kernel may reach another device: no remote copies, remote signals or barrier semaphores. Data moves between devices by JAX's collectives and lax.ppermute only.
A program may use at most 128 MiB of HBM per device.

```python
import math
import jax
import jax.numpy as jnp
from jax import lax

BANDS = 16
BS = 128
K = 24
RB = 6
ALEV = 64
AXD = 16
AY = 1024
STEPS = 2
VISIBLE = 48
BLOCK_ROWS = 192
PATCHES = 24576
BORDER_ROWS = 96
NXA = 128
NYA = 4096
N_DISTRICT = 8
N_BLK = 4


def draw_view_cols(key, part):
    key = jax.random.fold_in(key, 11)
    keys = jax.random.split(key, BLOCK_ROWS)
    table = jax.vmap(lambda single: jax.random.permutation(single, VISIBLE))(keys)
    return table[:, :K].astype(jnp.int32)


def draw_border_list(key, part):
    key = jax.random.fold_in(key, 23)
    keys = jax.random.split(key, BORDER_ROWS // (RB // 2))
    table = jax.vmap(lambda single: jax.random.permutation(single, RB))(keys)
    return table[:, :RB // 2].reshape(-1).astype(jnp.int32)


def draw_radiosity(key, part):
    key = jax.random.fold_in(key, 37)
    first, second = jax.random.split(key)
    level = jnp.exp(jax.random.uniform(first, (BANDS, BLOCK_ROWS, 1), jnp.float32, jnp.log(0.2), jnp.log(5.0)))
    rough = jax.random.uniform(second, (BANDS, BLOCK_ROWS, BS), jnp.float32, 0.5, 1.5)
    return (level * rough).reshape(BANDS, PATCHES).astype(jnp.bfloat16)


def set_ends(array, key, least, high):
    spot = [jax.random.randint(jax.random.fold_in(key, axis), (), 0, length) for axis, length in enumerate(array.shape)]
    longest = array.shape.index(max(array.shape))
    beside = spot[:longest] + [(spot[longest] + 1) % array.shape[longest]] + spot[longest + 1:]
    return array.at[tuple(spot)].set(least).at[tuple(beside)].set(high)


def block_scale(stream_key, shape, pieces, smallest, largest):
    factor_of, own = 1.0, jax.random.fold_in(stream_key, 6)
    for axis_at, parts in pieces:
        heights = jnp.exp(jax.random.uniform(jax.random.fold_in(own, axis_at), (parts,), jnp.float32, smallest / len(pieces), largest / len(pieces)))
        factor_of = factor_of * jnp.repeat(heights, shape[axis_at] // parts).reshape([-1 if axis == axis_at else 1 for axis in range(len(shape))])
    return factor_of


def centred(key, shape, deviation, most, cuts=(), kind=jnp.bfloat16):
    level = block_scale(key, shape, cuts, -0.22, 0.18) if cuts else 1.0
    entries = jax.random.normal(key, shape, jnp.float32) * deviation * level
    return jnp.minimum(jnp.maximum(entries, -most), most).astype(kind)


def setup_inputs(seed: int = 0) -> dict:
    splits = jax.random.split(jax.random.key(seed), 11)
    return {
        "view_factor": jnp.clip(0.00064849854 * jax.random.uniform(splits[0], (BLOCK_ROWS, K, BS, BS), jnp.float32) ** block_scale(splits[0], (BLOCK_ROWS, K, BS, BS), ((0, 32),), -0.2, 0.2), 0.0, 0.00064849854).astype(jnp.bfloat16),
        "view_cols": draw_view_cols(jax.random.fold_in(splits[10], 71), 0),
        "border_list": draw_border_list(jax.random.fold_in(splits[10], 71), 0),
        "radiosity": draw_radiosity(jax.random.fold_in(splits[10], 71), 0),
        "reflectance": jnp.clip(0.29882812 + 0.5996094 * jax.random.uniform(splits[4], (BANDS, PATCHES), jnp.float32) ** block_scale(splits[4], (BANDS, PATCHES), ((1, 32),), -0.2, 0.2), 0.29882812, 0.8984375).astype(jnp.bfloat16),
        "emissivity": jnp.clip(0.6 + 0.38 * jax.random.uniform(splits[5], (PATCHES,), jnp.float32) ** block_scale(splits[5], (PATCHES,), ((0, 32),), -0.2, 0.2), 0.6, 0.98),
        "band_weight": jnp.clip(jnp.exp(jax.random.uniform(splits[6], (BANDS,), jnp.float32, math.log(0.1), math.log(0.6))), 0.1, 0.6),
        "surface_temp": jnp.clip(0.8 + 0.49999994 * jax.random.uniform(splits[7], (PATCHES,), jnp.float32) ** block_scale(splits[7], (PATCHES,), ((0, 32),), -0.2, 0.2), 0.8, 1.3),
        "patch_cell": set_ends(jax.random.randint(splits[8], (PATCHES,), 0, AXD * AY), jax.random.fold_in(splits[8], 1), 0, (AXD * AY) - 1).astype(jnp.int32),
        "air": centred(splits[9], (ALEV, NXA, NYA), 1.0, 6.0, ((1, 8), (2, 4)), jnp.float32),
    }


KAPPA = 0.15
GAIN = 0.02
COUPLE = 0.2
HEAT = 1.0


def stencil_step(padded):
    vertical = jnp.pad(padded, ((1, 1), (0, 0), (0, 0)))
    center = padded[:, 1:-1, 1:-1]
    beside_all = padded[:, 2:, 1:-1] + padded[:, :-2, 1:-1]
    beside_all = beside_all + padded[:, 1:-1, 2:] + padded[:, 1:-1, :-2]
    beside_all = beside_all + vertical[2:, 1:-1, 1:-1] + vertical[:-2, 1:-1, 1:-1]
    return center + KAPPA * (beside_all - 6.0 * center)


def reference(view_factor, view_cols, border_list, radiosity, reflectance, emissivity, band_weight, surface_temp, patch_cell, air):
    half = RB // 2
    device_count = BLOCK_ROWS // RB
    rows = jnp.arange(BLOCK_ROWS, dtype=jnp.int32)
    district = (rows // RB) // N_BLK
    owner = view_cols // (2 * RB)
    slot = view_cols % (2 * RB)
    border_table = border_list.reshape(device_count, half)
    own_index = (district[:, None] * N_BLK + owner) * RB + slot
    left_dev = (district[:, None] - 1) * N_BLK + owner
    left_pos = jnp.clip(slot - RB, 0, half - 1)
    left_index = left_dev * RB + border_table[jnp.clip(left_dev, 0, device_count - 1), left_pos]
    right_dev = (district[:, None] + 1) * N_BLK + owner
    right_pos = jnp.clip(slot - RB - half, 0, half - 1)
    right_index = right_dev * RB + border_table[jnp.clip(right_dev, 0, device_count - 1), right_pos]
    is_own = slot < RB
    is_left = (slot >= RB) & (slot < RB + half)
    is_right = slot >= RB + half
    usable = is_own | (is_left & (district[:, None] >= 1)) | (is_right & (district[:, None] < N_DISTRICT - 1))
    chosen = jnp.where(is_own, own_index, jnp.where(is_left, left_index, right_index))
    chosen = jnp.where(usable, chosen, 0).astype(jnp.int32)
    blocks = radiosity.reshape(BANDS, BLOCK_ROWS, BS)

    def one_row(items):
        factors, picks, keep = items
        selected = jnp.take(blocks, picks, axis=1).astype(jnp.float32)
        selected = jnp.where(keep[None, :, None], selected, 0.0)
        return jnp.einsum("bkj,kij->bi", selected, factors.astype(jnp.float32))

    irradiance = lax.map(one_row, (view_factor, chosen, usable))
    irradiance = jnp.transpose(irradiance, (1, 0, 2)).reshape(BANDS, PATCHES)
    squared = surface_temp * surface_temp
    emission = emissivity[None, :] * band_weight[:, None] * (squared * squared)[None, :]
    albedo = reflectance.astype(jnp.float32)
    radiosity_next = emission + albedo * irradiance
    patches = jnp.arange(PATCHES, dtype=jnp.int32)
    device = patches // (RB * BS)
    xpos = (device // N_BLK) * AXD + patch_cell // AY
    ypos = (device % N_BLK) * AY + patch_cell % AY
    air_cell = air[0][xpos, ypos]
    absorbed = jnp.sum((1.0 - albedo) * irradiance, axis=0)
    emitted = jnp.sum(emission, axis=0)
    surface_next = surface_temp + GAIN * (absorbed - emitted) - COUPLE * (surface_temp - 1.0 - air_cell)
    field = air
    for step in range(STEPS):
        field = stencil_step(jnp.pad(field, ((0, 0), (1, 1), (1, 1))))
    flux = COUPLE * (surface_next - 1.0 - air_cell)
    source = jnp.zeros((NXA, NYA), jnp.float32).at[xpos, ypos].add(flux)
    air_next = field.at[0].add(HEAT * source)
    return radiosity_next, surface_next, air_next
```

```python
import functools

import jax
import jax.numpy as jnp
from jax import lax
from jax.experimental import pallas as pl
from jax.experimental.pallas import tpu as pltpu
from jax.sharding import PartitionSpec as P

KAPPA = 0.15
GAIN = 0.02
COUPLE = 0.2
HEAT = 1.0
CENTRE = (1.0 - 6.0 * KAPPA) / KAPPA
SQUARE = KAPPA * KAPPA

F32 = jnp.float32
BF16 = jnp.bfloat16
LANES = 128
VMEM = pltpu.VMEM
SMEM = pltpu.SMEM
DMA = pltpu.SemaphoreType.DMA
PACK_COST, ROWS_COST, JOIN_COST, MAIN_COST = 2, 2, 1, 8


def params(mebibytes):
    return pltpu.CompilerParams(vmem_limit_bytes=mebibytes << 20)


def cost(microseconds):
    return pl.CostEstimate(flops=0, bytes_accessed=microseconds * 3_000_000, transcendentals=0)


def in_hbm(value):
    return pltpu.with_memory_space_constraint(value, pltpu.HBM)


WHOLE = pl.BlockSpec(memory_space=VMEM)
PLACE = pl.BlockSpec(memory_space=pl.ANY)


def iota(shape, axis):
    return lax.broadcasted_iota(jnp.int32, shape, axis)


def split(value, pieces):
    out = []
    for _ in range(pieces):
        piece = value.astype(BF16)
        out.append(piece)
        value = value - piece.astype(F32)
    return out


def plane_neighbours(load, tiles):
    centre = [load(i) for i in range(tiles)]
    rows = centre[0].shape[0]
    lane = iota((rows, LANES), 1)
    row = iota((rows, LANES), 0)
    right = [pltpu.roll(c, 1, 1) for c in centre]
    left = [pltpu.roll(c, LANES - 1, 1) for c in centre]
    zero = jnp.zeros((rows, LANES), F32)
    for i, c in enumerate(centre):
        total = jnp.where(lane == 0, right[i - 1] if i else zero, right[i])
        total = total + jnp.where(
            lane == LANES - 1, left[i + 1] if i + 1 < tiles else zero, left[i]
        )
        total = total + jnp.where(row == 0, 0.0, pltpu.roll(c, 1, 0))
        total = total + jnp.where(row == rows - 1, 0.0, pltpu.roll(c, rows - 1, 0))
        yield c, total


def pack_kernel(
    border_ref,
    radiosity_ref,
    air_ref,
    near_small,
    far_small,
    own_ref,
    border,
    blocks_of,
    ends,
    sem,
    end_sem,
):
    levels, depth, width = air_ref.shape
    blocks = radiosity_ref.shape[1] // LANES
    borders = border_ref.shape[0]
    odd = lax.rem(lax.axis_index("district"), 2)
    edge = [
        pltpu.make_async_copy(
            air_ref.at[:, :, pl.ds(at, LANES)], ends.at[j], end_sem.at[j]
        )
        for j, at in enumerate((0, width - LANES))
    ]
    first = [
        pltpu.make_async_copy(border_ref, border, sem.at[0]),
        pltpu.make_async_copy(radiosity_ref, blocks_of, sem.at[1]),
    ]
    for c in edge + first:
        c.start()
    for c in first:
        c.wait()
    for s in range(blocks):
        own_ref[s] = blocks_of[:, s * LANES : (s + 1) * LANES]
    for s in range(borders):
        tile = own_ref[border[s]]
        near_small[s] = tile
        far_small[s] = tile
    place = iota((depth, LANES), 1) // 2
    corner_rows = [[], []]
    for j in range(2):
        edge[j].wait()
        packed = jnp.zeros((depth, LANES), F32)
        for z in range(levels):
            tile = ends[j, z]
            turn = (2 * z + 2 * j) % LANES
            packed = jnp.where(place == z, pltpu.roll(tile, turn, 1) if turn else tile, packed)
        for n, piece in enumerate(split(packed, 2)):
            own_ref[blocks + 2 * j + n] = piece
            wide = piece.astype(F32)
            corner_rows[0].append(wide[0:1])
            corner_rows[1].append(wide[depth - 1 : depth])
    sub = iota((16, LANES), 0)
    for which, small in enumerate((near_small, far_small)):
        last = (odd == 0) if which == 0 else (odd == 1)
        corner = jnp.zeros((16, LANES), F32)
        for n in range(4):
            row = jnp.where(last, corner_rows[1][n], corner_rows[0][n])
            corner = jnp.where(sub == n, row, corner)
        small[borders] = corner.astype(BF16)


def pack(border_list, radiosity, air):
    levels, depth, _ = air.shape
    blocks = radiosity.shape[1] // LANES
    borders = border_list.shape[0]
    small = jax.ShapeDtypeStruct((borders + 1, 16, LANES), BF16)
    own = jax.ShapeDtypeStruct((blocks + 4, 16, LANES), BF16)
    return pl.pallas_call(
        pack_kernel,
        out_shape=(small, small, own),
        in_specs=[PLACE] * 3,
        out_specs=(WHOLE,) * 3,
        scratch_shapes=[
            SMEM(border_list.shape, border_list.dtype),
            VMEM(radiosity.shape, BF16),
            VMEM((2, levels, depth, LANES), F32),
            DMA((2,)),
            DMA((2,)),
        ],
        compiler_params=params(8),
        cost_estimate=cost(PACK_COST),
        name="pack",
    )(in_hbm(border_list), in_hbm(radiosity), in_hbm(air))


def rows_kernel(air_ref, near_rows, far_rows, slabs, sem):
    levels, depth, width = air_ref.shape
    tiles = width // LANES
    odd = lax.rem(lax.axis_index("district"), 2)
    copies = [
        pltpu.make_async_copy(air_ref.at[:, r, :], slabs.at[i], sem.at[i])
        for i, r in enumerate((depth - 1, depth - 2, 0, 1))
    ]
    for c in copies:
        c.start()
    for c in copies:
        c.wait()
    for which, rows in enumerate((near_rows, far_rows)):
        base = 2 * (odd if which == 0 else 1 - odd)

        def lost(i):
            value = slabs[base, :, i * LANES : (i + 1) * LANES]
            return value - value.astype(BF16).astype(F32)

        for i, (c, around) in enumerate(plane_neighbours(lost, tiles)):
            at = slice(i * LANES, (i + 1) * LANES)
            rows[0, :, at] = slabs[base, :, at].astype(BF16)
            rows[1, :, at] = (slabs[base + 1, :, at] + CENTRE * 2.0 * c + 2.0 * around).astype(BF16)


def rows(air):
    levels, _, width = air.shape
    out = jax.ShapeDtypeStruct((2, levels, width), BF16)
    return pl.pallas_call(
        rows_kernel,
        out_shape=(out, out),
        in_specs=[PLACE],
        out_specs=(WHOLE, WHOLE),
        scratch_shapes=[VMEM((4, levels, width), F32), DMA((4,))],
        compiler_params=params(8),
        cost_estimate=cost(ROWS_COST),
        name="rows",
    )(in_hbm(air))


def join_kernel(own_ref, near_ref, far_ref, rows_ref, out_ref, rows_out):
    odd = lax.rem(lax.axis_index("district"), 2)
    borders = near_ref.shape[0] - 1
    blocks = own_ref.shape[0] - 4
    rows_out[...] = rows_ref[...]
    for s in range(blocks):
        out_ref[s] = own_ref[s]
    for s in range(4):
        out_ref[blocks + 2 * borders + 2 + s] = own_ref[blocks + s]
    for s in range(borders + 1):
        before = jnp.where(odd == 1, near_ref[s].astype(F32), far_ref[s].astype(F32)).astype(BF16)
        after = jnp.where(odd == 1, far_ref[s].astype(F32), near_ref[s].astype(F32)).astype(BF16)
        at = blocks + s if s < borders else blocks + 2 * borders
        out_ref[at] = before
        out_ref[at + (borders if s < borders else 1)] = after


def join(own, near, far, rows):
    count = own.shape[0] + 2 * near.shape[0]
    return pl.pallas_call(
        join_kernel,
        out_shape=(
            jax.ShapeDtypeStruct((count, 16, LANES), BF16),
            jax.ShapeDtypeStruct(rows.shape, BF16),
        ),
        in_specs=[WHOLE] * 4,
        out_specs=(WHOLE, WHOLE),
        compiler_params=params(8),
        cost_estimate=cost(JOIN_COST),
        name="join",
    )(own, near, far, rows)


def main_kernel(
    cols_ref,
    weight_ref,
    own_ref,
    one_ref,
    two_ref,
    three_ref,
    reflectance_ref,
    emissivity_ref,
    temp_ref,
    cell_ref,
    view_ref,
    air_ref,
    radiosity_out,
    surface_out,
    air_out,
    edge_out,
    once,
    twice,
    pieces,
    ends,
    surface_buf,
    out_sem,
    edge_sem,
    surface_sem,
    *,
    chunk,
):
    levels, depth, width = air_ref.shape
    tiles = width // LANES
    row_blocks, nonzero = view_ref.shape[0], view_ref.shape[1]
    chunks = levels // chunk
    district = lax.axis_index("district")
    blk = lax.axis_index("blk")
    districts = lax.axis_size("district")
    blks = lax.axis_size("blk")
    flag = lambda cond: jnp.where(cond, 1.0, 0.0).astype(F32)
    has_top, has_bottom = flag(district > 0), flag(district < districts - 1)
    has_left, has_right = flag(blk > 0), flag(blk < blks - 1)

    visible = own_ref.shape[0] - 6
    for n, ref in enumerate((own_ref, one_ref, two_ref, three_ref)):
        for s in range(visible):
            pieces[n * visible + s] = ref[s]

    def pair(ref, at):
        return ref[at].astype(F32) + ref[at + 1].astype(F32)

    sub = iota((depth, LANES), 0)
    lane = iota((depth, LANES), 1)
    even = lax.rem(blk, 2) == 0
    col_at = visible + 2
    left_cols = jnp.where(even, pair(three_ref, col_at + 2), pair(one_ref, col_at + 2)) * has_left
    right_cols = jnp.where(even, pair(one_ref, col_at), pair(three_ref, col_at)) * has_right

    def corner(left_side, top):
        at = visible + (0 if top else 1)
        one, three = one_ref[at].astype(F32), three_ref[at].astype(F32)
        value = jnp.where(even, three, one) if left_side else jnp.where(even, one, three)
        value = value * (has_left if left_side else has_right)
        k = 2 if left_side else 0
        row = value[k : k + 1] + value[k + 1 : k + 2]
        return pltpu.roll(row, LANES - 1, 1) if left_side else row

    own_left, own_right = pair(own_ref, col_at), pair(own_ref, col_at + 2)
    for side in range(2):
        if side == 0:
            first, second = pltpu.roll(left_cols, LANES - 1, 1), left_cols
            inner, has = own_left, has_left
        else:
            first, second = right_cols, pltpu.roll(right_cols, LANES - 1, 1)
            inner, has = pltpu.roll(own_right, LANES - 1, 1), has_right
        top, bottom = (corner(side == 0, up) for up in (True, False))
        around = jnp.where(sub == 0, 2.0 * top, pltpu.roll(first, 1, 0))
        around = around + jnp.where(sub == depth - 1, 2.0 * bottom, pltpu.roll(first, depth - 1, 0))
        around = around + jnp.where(lane < 2, 0.0, pltpu.roll(first, 2, 1))
        around = around + jnp.where(lane >= 2 * levels - 2, 0.0, pltpu.roll(first, LANES - 2, 1))
        ends[side, 0] = first
        ends[side, 1] = CENTRE * first + around + second + inner * has

    half = depth // 2
    halves = depth // half
    sub8 = iota((half, LANES), 0)
    lane8 = iota((half, LANES), 1)
    first_lane, last_lane = lane8 == 0, lane8 == LANES - 1
    first_row, last_row = sub8 == 0, sub8 == half - 1
    zero = jnp.zeros((half, LANES), F32)

    def stencil(z, src, dst, which):
        turn = lax.rem(LANES - 2 * z, LANES)
        below, above = jnp.maximum(z - 1, 0), jnp.minimum(z + 1, levels - 1)
        under, over = flag(z > 0), flag(z < levels - 1)
        at = [slice(t * LANES, (t + 1) * LANES) for t in range(tiles)]
        at_x = [slice(x * half, (x + 1) * half) for x in range(halves)]
        centre = [[src[z, i, j] for j in at] for i in at_x]
        down = [[pltpu.roll(c, 1, 0) for c in row] for row in centre]
        up = [[pltpu.roll(c, half - 1, 0) for c in row] for row in centre]
        for x in range(halves):
            fore = [pltpu.roll(c, 1, 1) for c in centre[x]]
            back = [pltpu.roll(c, LANES - 1, 1) for c in centre[x]]
            column = [ends[s, which, at_x[x]] for s in range(2)]
            enter = pltpu.roll(column[0], turn, 1)
            leave = pltpu.roll(column[1], lax.rem(turn + LANES - 1, LANES), 1)
            for t in range(tiles):
                before, after = zero, zero
                if x:
                    before = down[x - 1][t]
                elif which:
                    before = air_ref[z, at_x[x], at[t]] * has_top
                if x + 1 < halves:
                    after = up[x + 1][t]
                elif which:
                    after = air_ref[z, at_x[x], at[t]] * has_bottom
                total = src[below, at_x[x], at[t]] * under + src[above, at_x[x], at[t]] * over
                total = total + jnp.where(first_row, before, down[x][t])
                total = total + jnp.where(last_row, after, up[x][t])
                total = total + jnp.where(first_lane, fore[t - 1] if t else enter, fore[t])
                total = total + jnp.where(
                    last_lane, back[t + 1] if t + 1 < tiles else leave, back[t]
                )
                total = total + CENTRE * centre[x][t]
                dst[z, at_x[x], at[t]] = SQUARE * total if which else total

    def first_step(z, carry):
        stencil(z, air_ref, once, 0)
        return carry

    def second_step(z, carry):
        stencil(z, once, twice, 1)
        return carry

    writes = []

    def write(k):
        c = pltpu.make_async_copy(
            twice.at[pl.ds(k * chunk, chunk)], air_out.at[pl.ds(k * chunk, chunk)], out_sem.at[k]
        )
        c.start()
        writes.append(c)

    lax.fori_loop(0, levels, first_step, 0, unroll=UNROLL)
    for k in range(chunks):
        lax.fori_loop(k * chunk, (k + 1) * chunk, second_step, 0, unroll=UNROLL)
        if k:
            write(k)

    blocks = []
    for r in range(row_blocks):
        picked = []
        for k in range(nonzero):
            c = cols_ref[r, k]
            owner = c // visible
            picked.append(pieces[jnp.bitwise_xor(owner, blk) * visible + (c - owner * visible)])
        blocks.append(
            lax.dot_general(
                jnp.concatenate(picked, axis=1),
                jnp.concatenate([view_ref[r, k] for k in range(nonzero)], axis=1),
                (((1,), (1,)), ((), ())),
                preferred_element_type=F32,
            )
        )
    irradiance = jnp.concatenate(blocks, axis=1)

    ground = jnp.concatenate([air_ref[0, :, t * LANES : (t + 1) * LANES] for t in range(tiles)], axis=0)
    cell = cell_ref[...]
    patches = cell.shape[1]
    x_of, y_of = cell // width, cell % width
    high = (y_of // LANES) * depth + x_of
    low = y_of % LANES
    spots = iota((LANES, patches), 0)
    at_low = jnp.where(spots == low, 1.0, 0.0).astype(BF16)
    at_high = spots == high
    picked = sum(
        jnp.dot(piece, at_low, preferred_element_type=F32) for piece in split(ground, 3)
    )
    air_cell = jnp.sum(jnp.where(at_high, picked, 0.0), axis=0, keepdims=True)
    temp = temp_ref[...]
    squared = temp * temp
    emission = weight_ref[...] * (emissivity_ref[...] * (squared * squared))
    albedo = reflectance_ref[...].astype(F32)
    radiosity_out[...] = emission + albedo * irradiance
    absorbed = jnp.sum((1.0 - albedo) * irradiance, axis=0, keepdims=True)
    emitted = jnp.sum(emission, axis=0, keepdims=True)
    surface = temp + GAIN * (absorbed - emitted) - COUPLE * (temp - 1.0 - air_cell)
    surface_buf[...] = surface
    surface_copy = pltpu.make_async_copy(surface_buf.at[0], surface_out, surface_sem)
    surface_copy.start()
    writes.append(surface_copy)
    flux = HEAT * (COUPLE * (surface - 1.0 - air_cell))
    source = sum(
        lax.dot_general(
            jnp.where(at_high, piece.astype(F32), 0.0).astype(BF16),
            at_low,
            (((1,), (1,)), ((), ())),
            preferred_element_type=F32,
        )
        for piece in split(flux, 3)
    )
    for t in range(tiles):
        at = slice(t * LANES, (t + 1) * LANES)
        twice[0, :, at] = twice[0, :, at] + source[t * depth : (t + 1) * depth]
    write(0)
    for i, x in enumerate((0, 1, depth - 2, depth - 1)):
        c = pltpu.make_async_copy(twice.at[:, x, :], edge_out.at[i], edge_sem.at[i])
        c.start()
        writes.append(c)
    for c in writes:
        c.wait()


UNROLL = 4


def main(cols, weight, own, one, two, three, reflectance, emissivity, temp, cell, view, air):
    levels, depth, width = air.shape
    chunk = levels // 4
    bands, patches = reflectance.shape
    visible = own.shape[0] - 6
    return pl.pallas_call(
        functools.partial(main_kernel, chunk=chunk),
        out_shape=(
            jax.ShapeDtypeStruct((bands, patches), F32),
            jax.ShapeDtypeStruct((patches,), F32),
            jax.ShapeDtypeStruct(air.shape, F32),
            jax.ShapeDtypeStruct((4, levels, width), F32),
        ),
        in_specs=[pl.BlockSpec(memory_space=SMEM)] + [WHOLE] * 11,
        out_specs=(WHOLE, PLACE, PLACE, WHOLE),
        scratch_shapes=[
            VMEM(air.shape, F32),
            VMEM(air.shape, F32),
            VMEM((4 * visible, 16, LANES), BF16),
            VMEM((2, 2, depth, LANES), F32),
            VMEM((1, patches), F32),
            DMA((levels // chunk,)),
            DMA((4,)),
            DMA,
        ],
        compiler_params=params(32),
        cost_estimate=cost(MAIN_COST),
        name="main",
    )(cols, weight, own, one, two, three, reflectance, emissivity, temp, cell, view, air)


def finish_kernel(air_ref, edge_ref, near_ref, far_ref, out_ref, slabs, sem):
    del air_ref
    levels, width = near_ref.shape[1], near_ref.shape[2]
    depth = out_ref.shape[1]
    tiles = width // LANES
    odd = lax.rem(lax.axis_index("district"), 2)
    copies = []
    for side in range(2):
        use_near = (odd == 1) if side == 0 else (odd == 0)

        def received(k, i):
            at = slice(i * LANES, (i + 1) * LANES)
            return jnp.where(use_near, near_ref[k, :, at].astype(F32), far_ref[k, :, at].astype(F32))

        outer, inner = (0, 1) if side == 0 else (3, 2)
        for i, (c, around) in enumerate(plane_neighbours(functools.partial(received, 0), tiles)):
            at = slice(i * LANES, (i + 1) * LANES)
            reach = (2.0 * CENTRE) * c + 2.0 * around + received(1, i)
            slabs[outer, :, at] = edge_ref[outer, :, at] + SQUARE * reach
            slabs[inner, :, at] = edge_ref[inner, :, at] + SQUARE * c
        for i in (outer, inner):
            x = (0, 1, depth - 2, depth - 1)[i]
            c = pltpu.make_async_copy(slabs.at[i], out_ref.at[:, x, :], sem.at[i])
            c.start()
            copies.append(c)
    for c in copies:
        c.wait()


def finish(air, edge, near, far):
    return pl.pallas_call(
        finish_kernel,
        out_shape=jax.ShapeDtypeStruct(air.shape, F32),
        in_specs=[PLACE, WHOLE, WHOLE, WHOLE],
        out_specs=PLACE,
        scratch_shapes=[VMEM(edge.shape, F32), DMA((4,))],
        input_output_aliases={0: 0},
        compiler_params=params(8),
        name="finish",
    )(in_hbm(air), edge, near, far)


def swap(value, axis, pairs):
    return lax.ppermute(value, axis, [p for a, b in pairs for p in ((a, b), (b, a))])


def body(
    view_factor,
    view_cols,
    border_list,
    radiosity,
    reflectance,
    emissivity,
    band_weight,
    surface_temp,
    patch_cell,
    air,
):
    districts, blks = lax.axis_size("district"), lax.axis_size("blk")
    near_pairs = [(i, i + 1) for i in range(0, districts - 1, 2)]
    far_pairs = [(i, i + 1) for i in range(1, districts - 1, 2)]
    near_small, far_small, own = pack(border_list, radiosity, air)
    near_rows, far_rows = rows(air)
    near_small = swap(near_small, "district", near_pairs)
    far_small = swap(far_small, "district", far_pairs)
    near_rows = swap(near_rows, "district", near_pairs)
    own, far_rows = join(own, near_small, far_small, far_rows)
    far_rows = swap(far_rows, "district", far_pairs)
    one, two, three = (
        swap(own, "blk", [(i, i ^ k) for i in range(blks) if i < i ^ k]) for k in (1, 2, 3)
    )
    radiosity_next, surface_next, air_next, edge = main(
        view_cols,
        band_weight.reshape(-1, 1),
        own,
        one,
        two,
        three,
        reflectance,
        emissivity.reshape(1, -1),
        surface_temp.reshape(1, -1),
        patch_cell.reshape(1, -1),
        view_factor,
        air,
    )
    air_next = finish(air_next, edge, near_rows, far_rows)
    return radiosity_next, surface_next, air_next


def solution(mesh):
    in_specs = (
        P(("district", "blk"), None, None, None),
        P(("district", "blk"), None),
        P(("district", "blk")),
        P(None, ("district", "blk")),
        P(None, ("district", "blk")),
        P(("district", "blk")),
        P(),
        P(("district", "blk")),
        P(("district", "blk")),
        P(None, "district", "blk"),
    )
    out_specs = (P(None, ("district", "blk")), P(("district", "blk")), P(None, "district", "blk"))
    return jax.shard_map(body, mesh=mesh, in_specs=in_specs, out_specs=out_specs, check_vma=False)
```

```python
import functools

import jax
import jax.numpy as jnp
from jax import lax
from jax.experimental import pallas as pl
from jax.experimental.pallas import tpu as pltpu
from jax.sharding import PartitionSpec as P

KAPPA = 0.15
GAIN = 0.02
COUPLE = 0.2
HEAT = 1.0
CENTRE = (1.0 - 6.0 * KAPPA) / KAPPA
SQUARE = KAPPA * KAPPA

F32 = jnp.float32
BF16 = jnp.bfloat16
LANES = 128
VMEM = pltpu.VMEM
SMEM = pltpu.SMEM
DMA = pltpu.SemaphoreType.DMA
PACK_COST, ROWS_COST, JOIN_COST, FIRST_COST, SECOND_COST, MAIN_COST = 2, 2, 1, 3, 3, 4


def params(mebibytes):
    return pltpu.CompilerParams(vmem_limit_bytes=mebibytes << 20)


def cost(microseconds):
    return pl.CostEstimate(flops=int(microseconds * 1_000_000_000), bytes_accessed=0, transcendentals=0)


def in_hbm(value):
    return pltpu.with_memory_space_constraint(value, pltpu.HBM)


WHOLE = pl.BlockSpec(memory_space=VMEM)
PLACE = pl.BlockSpec(memory_space=pl.ANY)


def iota(shape, axis):
    return lax.broadcasted_iota(jnp.int32, shape, axis)


def flag(condition):
    return jnp.where(condition, 1.0, 0.0).astype(F32)


def split(value, pieces):
    out = []
    for _ in range(pieces):
        piece = value.astype(BF16)
        out.append(piece)
        value = value - piece.astype(F32)
    return out


def plane_neighbours(load, tiles):
    centre = [load(i) for i in range(tiles)]
    rows = centre[0].shape[0]
    lane = iota((rows, LANES), 1)
    row = iota((rows, LANES), 0)
    right = [pltpu.roll(c, 1, 1) for c in centre]
    left = [pltpu.roll(c, LANES - 1, 1) for c in centre]
    zero = jnp.zeros((rows, LANES), F32)
    for i, c in enumerate(centre):
        total = jnp.where(lane == 0, right[i - 1] if i else zero, right[i])
        total = total + jnp.where(
            lane == LANES - 1, left[i + 1] if i + 1 < tiles else zero, left[i]
        )
        total = total + jnp.where(row == 0, 0.0, pltpu.roll(c, 1, 0))
        total = total + jnp.where(row == rows - 1, 0.0, pltpu.roll(c, rows - 1, 0))
        yield c, total


def pack_kernel(
    border_ref,
    radiosity_ref,
    air_ref,
    near_small,
    far_small,
    own_ref,
    border,
    blocks_of,
    ends,
    spread,
    sem,
    end_sem,
):
    levels, depth, width = air_ref.shape
    blocks = radiosity_ref.shape[1] // LANES
    borders = border_ref.shape[0]
    odd = lax.rem(lax.axis_index("district"), 2)
    first = [
        pltpu.make_async_copy(border_ref, border, sem.at[0]),
        pltpu.make_async_copy(radiosity_ref, blocks_of, sem.at[1]),
    ]
    edge = [
        pltpu.make_async_copy(
            air_ref.at[:, x, pl.ds(y, LANES)], ends.at[i, j], end_sem.at[i, j]
        )
        for i, x in enumerate((0, depth - 1))
        for j, y in enumerate((0, width - LANES))
    ]
    for c in first + edge:
        c.start()
    spread[...] = jnp.zeros(spread.shape, F32)
    for c in first:
        c.wait()
    for s in range(blocks):
        own_ref[s] = blocks_of[:, s * LANES : (s + 1) * LANES]
    for s in range(borders):
        tile = own_ref[border[s]]
        near_small[s] = tile
        far_small[s] = tile
    for c in edge:
        c.wait()
    lane = iota((levels, LANES), 1)
    sub = iota((16, LANES), 0)
    corner = []
    for i in range(2):
        spread[i, pl.ds(0, levels, 2), :] = jnp.where(lane < LANES // 2, ends[i, 0], ends[i, 1])
        turned = spread[i].T
        tile = jnp.zeros((16, LANES), F32)
        for n, row in enumerate((turned[0:1], turned[LANES - 1 : LANES])):
            high = row.astype(BF16).astype(F32)
            tile = jnp.where(sub == 2 * n, high, tile)
            tile = jnp.where(sub == 2 * n + 1, row - high, tile)
        corner.append(tile)
    near_small[borders] = jnp.where(odd == 0, corner[1], corner[0]).astype(BF16)
    far_small[borders] = jnp.where(odd == 0, corner[0], corner[1]).astype(BF16)


def pack(border_list, radiosity, air):
    levels = air.shape[0]
    blocks = radiosity.shape[1] // LANES
    borders = border_list.shape[0]
    small = jax.ShapeDtypeStruct((borders + 1, 16, LANES), BF16)
    own = jax.ShapeDtypeStruct((blocks, 16, LANES), BF16)
    return pl.pallas_call(
        pack_kernel,
        out_shape=(small, small, own),
        in_specs=[PLACE] * 3,
        out_specs=(WHOLE,) * 3,
        scratch_shapes=[
            SMEM(border_list.shape, border_list.dtype),
            VMEM(radiosity.shape, BF16),
            VMEM((2, 2, levels, LANES), F32),
            VMEM((2, LANES, LANES), F32),
            DMA((2,)),
            DMA((2, 2)),
        ],
        compiler_params=params(8),
        cost_estimate=cost(PACK_COST),
        name="pack",
    )(in_hbm(border_list), in_hbm(radiosity), in_hbm(air))


def rows_kernel(air_ref, after_ref, near_rows, far_rows, columns, slabs, ends, sem, end_sem):
    del after_ref
    levels, depth, width = air_ref.shape
    tiles = width // LANES
    odd = lax.rem(lax.axis_index("district"), 2)
    edge = [
        pltpu.make_async_copy(air_ref.at[:, :, pl.ds(y, LANES)], ends.at[j], end_sem.at[j])
        for j, y in enumerate((0, width - LANES))
    ]
    copies = [
        pltpu.make_async_copy(air_ref.at[:, r, :], slabs.at[i], sem.at[i])
        for i, r in enumerate((depth - 1, depth - 2, 0, 1))
    ]
    for c in edge + copies:
        c.start()
    place = iota((depth, LANES), 1) // 2
    for j in range(2):
        edge[j].wait()
        packed = jnp.zeros((depth, LANES), F32)
        for z in range(levels):
            tile = ends[j, z]
            turn = (2 * z + 2 * j) % LANES
            packed = jnp.where(place == z, pltpu.roll(tile, turn, 1) if turn else tile, packed)
        for n, piece in enumerate(split(packed, 2)):
            columns[2 * j + n] = piece
    for c in copies:
        c.wait()
    for which, rows in enumerate((near_rows, far_rows)):
        base = 2 * (odd if which == 0 else 1 - odd)

        def lost(i):
            value = slabs[base, :, i * LANES : (i + 1) * LANES]
            return value - value.astype(BF16).astype(F32)

        for i, (c, around) in enumerate(plane_neighbours(lost, tiles)):
            at = slice(i * LANES, (i + 1) * LANES)
            rows[0, :, at] = slabs[base, :, at].astype(BF16)
            rows[1, :, at] = (slabs[base + 1, :, at] + CENTRE * 2.0 * c + 2.0 * around).astype(BF16)


def rows(air, after):
    levels, depth, width = air.shape
    out = jax.ShapeDtypeStruct((2, levels, width), BF16)
    return pl.pallas_call(
        rows_kernel,
        out_shape=(out, out, jax.ShapeDtypeStruct((4, depth, LANES), BF16)),
        in_specs=[PLACE, PLACE],
        out_specs=(WHOLE,) * 3,
        scratch_shapes=[
            VMEM((4, levels, width), F32),
            VMEM((2, levels, depth, LANES), F32),
            DMA((4,)),
            DMA((2,)),
        ],
        compiler_params=params(8),
        cost_estimate=cost(ROWS_COST),
        name="rows",
    )(in_hbm(air), after)


def join_kernel(own_ref, columns_ref, near_ref, far_ref, out_ref):
    odd = lax.rem(lax.axis_index("district"), 2)
    borders = near_ref.shape[0] - 1
    blocks = own_ref.shape[0]
    for s in range(blocks):
        out_ref[s] = own_ref[s]
    for s in range(4):
        out_ref[blocks + 2 * borders + 2 + s] = columns_ref[s]
    for s in range(borders + 1):
        before = jnp.where(odd == 1, near_ref[s].astype(F32), far_ref[s].astype(F32)).astype(BF16)
        after = jnp.where(odd == 1, far_ref[s].astype(F32), near_ref[s].astype(F32)).astype(BF16)
        at = blocks + s if s < borders else blocks + 2 * borders
        out_ref[at] = before
        out_ref[at + (borders if s < borders else 1)] = after


def join(own, columns, near, far):
    count = own.shape[0] + columns.shape[0] + 2 * near.shape[0]
    return pl.pallas_call(
        join_kernel,
        out_shape=jax.ShapeDtypeStruct((count, 16, LANES), BF16),
        in_specs=[WHOLE] * 4,
        out_specs=WHOLE,
        compiler_params=params(8),
        cost_estimate=cost(JOIN_COST),
        name="join",
    )(own, columns, near, far)


def stack_kernel(one_ref, two_ref, out_ref):
    part = one_ref.shape[0]
    for s in range(part):
        out_ref[s] = one_ref[s]
        out_ref[part + s] = two_ref[s]


def stack(one, two):
    return pl.pallas_call(
        stack_kernel,
        out_shape=jax.ShapeDtypeStruct((2 * one.shape[0], 16, LANES), BF16),
        in_specs=[WHOLE] * 2,
        out_specs=WHOLE,
        compiler_params=params(8),
        cost_estimate=cost(JOIN_COST),
        name="stack",
    )(one, two)


def cell_masks(cell_ref, depth, width):
    patches = cell_ref.shape[0]
    cell = cell_ref[...].reshape(1, patches)
    x_of, y_of = cell // width, cell % width
    spots = iota((LANES, patches), 0)
    at_low = jnp.where(spots == y_of % LANES, 1.0, 0.0).astype(BF16)
    return at_low, spots == (y_of // LANES) * depth + x_of


def stencil_level(z, src, store, beyond):
    levels, depth, width = src.shape
    tiles = width // LANES
    half = depth // 2
    sub = iota((half, LANES), 0)
    lane = iota((half, LANES), 1)
    zero = jnp.zeros((half, LANES), F32)
    below, above = jnp.maximum(z - 1, 0), jnp.minimum(z + 1, levels - 1)
    under, over = flag(z > 0), flag(z < levels - 1)
    at = [slice(t * LANES, (t + 1) * LANES) for t in range(tiles)]
    at_x = [slice(x * half, (x + 1) * half) for x in range(2)]
    centre = [[src[z, i, j] for j in at] for i in at_x]
    for x in range(2):
        fore = [pltpu.roll(c, 1, 1) for c in centre[x]]
        back = [pltpu.roll(c, LANES - 1, 1) for c in centre[x]]
        for t in range(tiles):
            c = centre[x][t]
            before = pltpu.roll(centre[0][t], 1, 0) if x else beyond(0, t)
            after = beyond(1, t) if x else pltpu.roll(centre[1][t], half - 1, 0)
            total = src[below, at_x[x], at[t]] * under + src[above, at_x[x], at[t]] * over
            total = total + jnp.where(sub == 0, before, pltpu.roll(c, 1, 0))
            total = total + jnp.where(sub == half - 1, after, pltpu.roll(c, half - 1, 0))
            total = total + jnp.where(lane == 0, fore[t - 1] if t else zero, fore[t])
            total = total + jnp.where(
                lane == LANES - 1, back[t + 1] if t + 1 < tiles else zero, back[t]
            )
            store(x, t, total + CENTRE * c)


def first_kernel(air_ref, after_ref, once):
    del after_ref
    levels, depth, _ = air_ref.shape
    half = depth // 2
    zero = jnp.zeros((half, LANES), F32)

    def level(z, carry):
        def store(x, t, total):
            once[z, x * half : (x + 1) * half, t * LANES : (t + 1) * LANES] = total

        stencil_level(z, air_ref, store, lambda x, t: zero)
        return carry

    lax.fori_loop(0, levels, level, 0, unroll=8)


def first(air, after):
    return pl.pallas_call(
        first_kernel,
        out_shape=jax.ShapeDtypeStruct(air.shape, F32),
        in_specs=[WHOLE, PLACE],
        out_specs=WHOLE,
        compiler_params=params(12),
        cost_estimate=cost(FIRST_COST),
        name="first",
    )(air, after)


def second_kernel(
    air_ref,
    once,
    cell_ref,
    air_out,
    ground_out,
    sides_out,
    edge_out,
    cell_out,
    result,
    out_sem,
    edge_sem,
    *,
    chunk,
):
    levels, depth, width = once.shape
    tiles = width // LANES
    half = depth // 2
    district = lax.axis_index("district")
    has_top, has_bottom = flag(district > 0), flag(district < lax.axis_size("district") - 1)
    at = [slice(t * LANES, (t + 1) * LANES) for t in range(tiles)]
    at_x = [slice(x * half, (x + 1) * half) for x in range(2)]

    def level(z, carry):
        def beyond(x, t):
            return air_ref[z, at_x[x], at[t]] * (has_bottom if x else has_top)

        def store(x, t, total):
            total = SQUARE * total
            result[z, at_x[x], at[t]] = total
            if t in (0, tiles - 1):
                sides_out[0 if t == 0 else 1, z, at_x[x]] = total

        stencil_level(z, once, store, beyond)
        return carry

    writes = []
    for k in range(levels // chunk):
        lax.fori_loop(k * chunk, (k + 1) * chunk, level, 0, unroll=8)
        span = pl.ds(k * chunk, chunk)
        lanes = pl.ds(LANES, width - 2 * LANES)
        fresh = [
            pltpu.make_async_copy(
                result.at[span, :, lanes], air_out.at[span, :, lanes], out_sem.at[k]
            )
        ]
        for i, x in enumerate((0, 1, depth - 2, depth - 1)):
            fresh.append(
                pltpu.make_async_copy(
                    result.at[span, x, lanes], edge_out.at[i, span], edge_sem.at[k, i]
                )
            )
        for c in fresh:
            c.start()
        writes += fresh
    ground_out[...] = result[0]
    at_low, at_high = cell_masks(cell_ref, depth, width)
    ground = jnp.concatenate([air_ref[0, :, j] for j in at], axis=0)
    picked = sum(
        jnp.dot(piece, at_low, preferred_element_type=F32) for piece in split(ground, 3)
    )
    cell_out[...] = jnp.sum(jnp.where(at_high, picked, 0.0), axis=0, keepdims=True)
    for c in writes:
        c.wait()


def second(air, once, cell):
    levels, depth, width = air.shape
    chunk = levels // 8
    return pl.pallas_call(
        functools.partial(second_kernel, chunk=chunk),
        out_shape=(
            jax.ShapeDtypeStruct(air.shape, F32),
            jax.ShapeDtypeStruct((depth, width), F32),
            jax.ShapeDtypeStruct((2, levels, depth, LANES), F32),
            jax.ShapeDtypeStruct((4, levels, width - 2 * LANES), F32),
            jax.ShapeDtypeStruct((1, cell.shape[0]), F32),
        ),
        in_specs=[WHOLE] * 3,
        out_specs=(PLACE,) + (WHOLE,) * 4,
        scratch_shapes=[VMEM(air.shape, F32), DMA((levels // chunk,)), DMA((levels // chunk, 4))],
        compiler_params=params(20),
        cost_estimate=cost(SECOND_COST),
        name="second",
    )(air, once, cell)


def main_kernel(
    cols_ref,
    weight_ref,
    mine_ref,
    theirs_ref,
    reflectance_ref,
    emissivity_ref,
    temp_ref,
    cell_ref,
    view_ref,
    air_cell_ref,
    ground_ref,
    sides_ref,
    next_ref,
    radiosity_out,
    surface_out,
    air_out,
    side_edge_out,
    source_out,
    ground_out,
    sides,
    pieces,
    radiosity_buf,
    surface_buf,
    out_sem,
    edge_sem,
    surface_sem,
):
    del next_ref
    levels, depth = sides_ref.shape[1:3]
    width = ground_ref.shape[1]
    tiles = width // LANES
    row_blocks, nonzero = view_ref.shape[0], view_ref.shape[1]
    blk = lax.axis_index("blk")
    blks = lax.axis_size("blk")
    has_left, has_right = flag(blk > 0), flag(blk < blks - 1)
    part = mine_ref.shape[0] // 2
    visible = part - 6
    for n, (ref, base) in enumerate(
        ((mine_ref, 0), (theirs_ref, 0), (mine_ref, part), (theirs_ref, part))
    ):
        for s in range(visible):
            pieces[n * visible + s] = ref[base + s]

    writes = []
    even = lax.rem(blk, 2) == 0

    def pair(ref, at):
        return ref[at].astype(F32) + ref[at + 1].astype(F32)

    def received(load):
        one, three = load(0), load(part)
        return jnp.where(even, three, one) * has_left, jnp.where(even, one, three) * has_right

    columns = [received(lambda base, n=n: pair(theirs_ref, base + visible + 2 + n)) for n in (0, 2)]
    corners = [received(lambda base, n=n: theirs_ref[base + visible + n].astype(F32)) for n in (0, 1)]
    sub = iota((depth, LANES), 0)
    lane = iota((depth, LANES), 1)
    half = depth // 2
    beside = []
    for side in range(2):
        k = 2 if side == 0 else 0
        shift = LANES - 1 if side == 0 else 0
        turn = lambda v: pltpu.roll(v, shift, 1) if shift else v
        near = turn(columns[1 - side][side])
        beyond = columns[1][0] if side == 0 else pltpu.roll(columns[0][1], LANES - 1, 1)
        own = pair(mine_ref, visible + 2 + 2 * side)
        own = own if side == 0 else pltpu.roll(own, LANES - 1, 1)
        top, bottom = (c[side][k : k + 1] + c[side][k + 1 : k + 2] for c in corners)
        around = jnp.where(sub == 0, top, pltpu.roll(near, 1, 0))
        around = around + jnp.where(sub == depth - 1, bottom, pltpu.roll(near, depth - 1, 0))
        around = around + jnp.where(lane < 2, 0.0, pltpu.roll(near, 2, 1))
        around = around + jnp.where(lane >= 2 * levels - 2, 0.0, pltpu.roll(near, LANES - 2, 1))
        outer = 2.0 * CENTRE * near + 2.0 * around + beyond + own * (has_right if side else has_left)
        if side == 0:
            value = jnp.where(lane % 2 == 0, outer, pltpu.roll(near, 1, 1))
        else:
            value = jnp.where(lane % 2 == 0, near, pltpu.roll(outer, 1, 1))
        beside.append(SQUARE * value)

    lane8 = iota((half, LANES), 1)
    both = [lane8 < 2, lane8 >= LANES - 2]

    def edges(z, carry):
        for side in range(2):
            turn = lax.rem(2 * LANES - 2 * z - 2 * side, LANES)
            for x in range(2):
                at = slice(x * half, (x + 1) * half)
                value = pltpu.roll(beside[side][at], turn, 1)
                sides[side, z, at] = sides_ref[side, z, at] + jnp.where(both[side], value, 0.0)
        return carry

    lax.fori_loop(0, levels, edges, 0, unroll=8)
    for side in range(2):
        lanes = pl.ds(side * (width - LANES), LANES)
        c = pltpu.make_async_copy(
            sides.at[side, pl.ds(1, levels - 1)],
            air_out.at[pl.ds(1, levels - 1), :, lanes],
            out_sem.at[side],
        )
        c.start()
        writes.append(c)
        for i, x in enumerate((0, 1, depth - 2, depth - 1)):
            c = pltpu.make_async_copy(
                sides.at[side, :, x, :], side_edge_out.at[side, i], edge_sem.at[side, i]
            )
            c.start()
            writes.append(c)
    blocks = []
    for r in range(row_blocks):
        picked = []
        for k in range(nonzero):
            c = cols_ref[r, k]
            owner = c // visible
            picked.append(pieces[jnp.bitwise_xor(owner, blk) * visible + (c - owner * visible)])
        blocks.append(
            lax.dot_general(
                jnp.concatenate(picked, axis=1),
                jnp.concatenate([view_ref[r, k] for k in range(nonzero)], axis=1),
                (((1,), (1,)), ((), ())),
                preferred_element_type=F32,
            )
        )
    irradiance = jnp.concatenate(blocks, axis=1)

    patches = cell_ref.shape[0]
    at_low, at_high = cell_masks(cell_ref, depth, width)
    air_cell = air_cell_ref[...]
    temp = temp_ref[...].reshape(1, patches)
    squared = temp * temp
    bands = reflectance_ref.shape[0]
    weight = jnp.zeros((bands, LANES), F32)
    for n in range(bands):
        weight = jnp.where(iota((bands, LANES), 0) == n, weight_ref[n], weight)
    weight = jnp.concatenate([weight] * (patches // LANES), axis=1)
    emission = weight * (emissivity_ref[...].reshape(1, patches) * (squared * squared))
    albedo = reflectance_ref[...].astype(F32)
    radiosity_buf[...] = emission + albedo * irradiance
    c = pltpu.make_async_copy(radiosity_buf, radiosity_out, surface_sem.at[1])
    c.start()
    writes.append(c)
    absorbed = jnp.sum((1.0 - albedo) * irradiance, axis=0, keepdims=True)
    emitted = jnp.sum(emission, axis=0, keepdims=True)
    surface = temp + GAIN * (absorbed - emitted) - COUPLE * (temp - 1.0 - air_cell)
    surface_buf[...] = surface
    c = pltpu.make_async_copy(surface_buf.at[0], surface_out, surface_sem.at[0])
    c.start()
    writes.append(c)
    flux = HEAT * (COUPLE * (surface - 1.0 - air_cell))
    source = sum(
        lax.dot_general(
            jnp.where(at_high, piece.astype(F32), 0.0).astype(BF16),
            at_low,
            (((1,), (1,)), ((), ())),
            preferred_element_type=F32,
        )
        for piece in split(flux, 3)
    )

    for t in range(tiles):
        at = slice(t * LANES, (t + 1) * LANES)
        here = source[t * depth : (t + 1) * depth]
        before = sides[0 if t == 0 else 1, 0] if t in (0, tiles - 1) else ground_ref[:, at]
        ground_out[:, at] = before + here
        for i, x in enumerate((0, 1, depth - 2, depth - 1)):
            source_out[i : i + 1, at] = here[x : x + 1]
    for c in writes:
        c.wait()


def main(
    cols, weight, mine, theirs, reflectance, emissivity, temp, cell, view, air_cell, ground, sides, following
):
    levels, depth = sides.shape[1:3]
    width = ground.shape[1]
    bands, patches = reflectance.shape
    visible = mine.shape[0] // 2 - 6
    return pl.pallas_call(
        main_kernel,
        out_shape=(
            jax.ShapeDtypeStruct((bands, patches), F32),
            jax.ShapeDtypeStruct((patches,), F32),
            jax.ShapeDtypeStruct(following.shape, F32),
            jax.ShapeDtypeStruct((2, 4, levels, LANES), F32),
            jax.ShapeDtypeStruct((4, width), F32),
            jax.ShapeDtypeStruct((depth, width), F32),
        ),
        in_specs=[pl.BlockSpec(memory_space=SMEM)] * 2 + [WHOLE] * 10 + [PLACE],
        out_specs=(PLACE, PLACE, PLACE, WHOLE, WHOLE, WHOLE),
        scratch_shapes=[
            VMEM(sides.shape, F32),
            VMEM((4 * visible, 16, LANES), BF16),
            VMEM((bands, patches), F32),
            VMEM((1, patches), F32),
            DMA((2,)),
            DMA((2, 4)),
            DMA((2,)),
        ],
        input_output_aliases={12: 2},
        compiler_params=params(20),
        cost_estimate=cost(MAIN_COST),
        name="main",
    )(
        cols,
        weight,
        mine,
        theirs,
        reflectance,
        emissivity,
        temp,
        cell,
        view,
        air_cell,
        ground,
        sides,
        in_hbm(following),
    )


def finish_kernel(
    air_ref, edge_ref, side_ref, source_ref, ground_ref, near_ref, far_ref, out_ref, slabs, sem
):
    del air_ref
    levels, width = near_ref.shape[1], near_ref.shape[2]
    depth = out_ref.shape[1]
    tiles = width // LANES
    odd = lax.rem(lax.axis_index("district"), 2)
    ground = iota((levels, LANES), 0) == 0
    copies = [
        pltpu.make_async_copy(ground_ref.at[x], out_ref.at[0, x], sem.at[2 + x])
        for x in range(2, depth - 2)
    ]
    for c in copies:
        c.start()
    for side in range(2):
        use_near = (odd == 1) if side == 0 else (odd == 0)

        def received(k, i):
            at = slice(i * LANES, (i + 1) * LANES)
            return jnp.where(use_near, near_ref[k, :, at].astype(F32), far_ref[k, :, at].astype(F32))

        def base(n, i):
            if i in (0, tiles - 1):
                value = side_ref[0 if i == 0 else 1, n]
            else:
                value = edge_ref[n, :, (i - 1) * LANES : i * LANES]
            return value + jnp.where(ground, source_ref[n : n + 1, i * LANES : (i + 1) * LANES], 0.0)

        outer, inner = (0, 1) if side == 0 else (3, 2)
        for i, (c, around) in enumerate(plane_neighbours(functools.partial(received, 0), tiles)):
            at = slice(i * LANES, (i + 1) * LANES)
            reach = (2.0 * CENTRE) * c + 2.0 * around + received(1, i)
            slabs[outer, :, at] = base(outer, i) + SQUARE * reach
            slabs[inner, :, at] = base(inner, i) + SQUARE * c
        for i in (outer, inner):
            x = (0, 1, depth - 2, depth - 1)[i]
            c = pltpu.make_async_copy(slabs.at[i], out_ref.at[:, x, :], sem.at[i])
            c.start()
            copies.append(c)
    for c in copies:
        c.wait()


def finish(air, edge, side, source, ground, near, far):
    levels, width = near.shape[1:]
    return pl.pallas_call(
        finish_kernel,
        out_shape=jax.ShapeDtypeStruct(air.shape, F32),
        in_specs=[PLACE] + [WHOLE] * 6,
        out_specs=PLACE,
        scratch_shapes=[VMEM((4, levels, width), F32), DMA((air.shape[1],))],
        input_output_aliases={0: 0},
        compiler_params=params(8),
        name="finish",
    )(in_hbm(air), edge, side, source, ground, near, far)


def swap(value, axis, pairs):
    return lax.ppermute(value, axis, [p for a, b in pairs for p in ((a, b), (b, a))])


def body(
    view_factor,
    view_cols,
    border_list,
    radiosity,
    reflectance,
    emissivity,
    band_weight,
    surface_temp,
    patch_cell,
    air,
):
    districts, blks = lax.axis_size("district"), lax.axis_size("blk")
    near_pairs = [(i, i + 1) for i in range(0, districts - 1, 2)]
    far_pairs = [(i, i + 1) for i in range(1, districts - 1, 2)]
    near_small, far_small, own = pack(border_list, radiosity, air)
    near_rows, far_rows, columns = rows(air, own)
    near_small = swap(near_small, "district", near_pairs)
    far_small = swap(far_small, "district", far_pairs)
    near_rows = swap(near_rows, "district", near_pairs)
    far_rows = swap(far_rows, "district", far_pairs)
    once = first(air, own)
    following, ground, sides, edge, air_cell = second(air, once, patch_cell)
    own = join(own, columns, near_small, far_small)
    across = swap(own, "blk", [(i, i ^ 2) for i in range(blks) if i < i ^ 2])
    mine = stack(own, across)
    theirs = swap(mine, "blk", [(i, i ^ 1) for i in range(blks) if i < i ^ 1])
    radiosity_next, surface_next, air_next, side, source, ground = main(
        view_cols,
        band_weight,
        mine,
        theirs,
        reflectance,
        emissivity,
        surface_temp,
        patch_cell,
        view_factor,
        air_cell,
        ground,
        sides,
        following,
    )
    air_next = finish(air_next, edge, side, source, ground, near_rows, far_rows)
    return radiosity_next, surface_next, air_next


def solution(mesh):
    in_specs = (
        P(("district", "blk"), None, None, None),
        P(("district", "blk"), None),
        P(("district", "blk")),
        P(None, ("district", "blk")),
        P(None, ("district", "blk")),
        P(("district", "blk")),
        P(),
        P(("district", "blk")),
        P(("district", "blk")),
        P(None, "district", "blk"),
    )
    out_specs = (P(None, ("district", "blk")), P(("district", "blk")), P(None, "district", "blk"))
    return jax.shard_map(body, mesh=mesh, in_specs=in_specs, out_specs=out_specs, check_vma=False)
```

```python
import functools

import jax
import jax.numpy as jnp
from jax import lax
from jax.experimental import pallas as pl
from jax.experimental.pallas import tpu as pltpu
from jax.sharding import PartitionSpec as P

KAPPA = 0.15
GAIN = 0.02
COUPLE = 0.2
HEAT = 1.0
CENTRE = (1.0 - 6.0 * KAPPA) / KAPPA
SQUARE = KAPPA * KAPPA

F32 = jnp.float32
BF16 = jnp.bfloat16
LANES = 128
VMEM = pltpu.VMEM
SMEM = pltpu.SMEM
DMA = pltpu.SemaphoreType.DMA
PACK_COST, COLUMNS_COST, ROWS_COST, JOIN_COST, HOLD_COST, FIRST_COST, SECOND_COST, MAIN_COST = 2, 0.1, 1, 1, 0.1, 1, 1, 1


def params(mebibytes):
    return pltpu.CompilerParams(vmem_limit_bytes=mebibytes << 20)


def cost(microseconds):
    return pl.CostEstimate(flops=int(microseconds * 1_000_000_000), bytes_accessed=0, transcendentals=0)


def in_hbm(value):
    return pltpu.with_memory_space_constraint(value, pltpu.HBM)


WHOLE = pl.BlockSpec(memory_space=VMEM)
PLACE = pl.BlockSpec(memory_space=pl.ANY)


def iota(shape, axis):
    return lax.broadcasted_iota(jnp.int32, shape, axis)


def flag(condition):
    return jnp.where(condition, 1.0, 0.0).astype(F32)


def split(value, pieces):
    out = []
    for _ in range(pieces):
        piece = value.astype(BF16)
        out.append(piece)
        value = value - piece.astype(F32)
    return out


def plane_neighbours(load, tiles):
    centre = [load(i) for i in range(tiles)]
    rows = centre[0].shape[0]
    lane = iota((rows, LANES), 1)
    row = iota((rows, LANES), 0)
    right = [pltpu.roll(c, 1, 1) for c in centre]
    left = [pltpu.roll(c, LANES - 1, 1) for c in centre]
    zero = jnp.zeros((rows, LANES), F32)
    for i, c in enumerate(centre):
        total = jnp.where(lane == 0, right[i - 1] if i else zero, right[i])
        total = total + jnp.where(
            lane == LANES - 1, left[i + 1] if i + 1 < tiles else zero, left[i]
        )
        total = total + jnp.where(row == 0, 0.0, pltpu.roll(c, 1, 0))
        total = total + jnp.where(row == rows - 1, 0.0, pltpu.roll(c, rows - 1, 0))
        yield c, total


def start_rows(air_ref, slabs, sem, last):
    depth = air_ref.shape[1]
    for i, r in enumerate((depth - 1, depth - 2) if last else (0, 1)):
        pltpu.make_async_copy(air_ref.at[:, r, :], slabs.at[i], sem.at[i]).start()


def wait_rows(air_ref, slabs, sem):
    for i in range(2):
        pltpu.make_async_copy(air_ref.at[:, i, :], slabs.at[i], sem.at[i]).wait()


def put_rows(slabs, out_ref):
    levels, width = slabs.shape[1:]
    tiles, parts = width // LANES, levels // 16

    def lost(i):
        value = slabs[0, :, i * LANES : (i + 1) * LANES]
        return value - value.astype(BF16).astype(F32)

    for i, (c, around) in enumerate(plane_neighbours(lost, tiles)):
        at = slice(i * LANES, (i + 1) * LANES)
        values = slabs[0, :, at], slabs[1, :, at] + CENTRE * 2.0 * c + 2.0 * around
        for k, value in enumerate(values):
            value = value.astype(BF16)
            for q in range(parts):
                out_ref[(k * tiles + i) * parts + q] = value[16 * q : 16 * q + 16]


def pack_kernel(
    border_ref,
    radiosity_ref,
    air_ref,
    near_out,
    far_small,
    own_ref,
    border,
    blocks_of,
    ends,
    spread,
    slabs,
    sem,
    end_sem,
    row_sem,
):
    levels, depth, width = air_ref.shape
    blocks = radiosity_ref.shape[1] // LANES
    borders = border_ref.shape[0]
    at_small = near_out.shape[0] - far_small.shape[0]
    odd = lax.rem(lax.axis_index("district"), 2)

    @pl.when(odd == 0)
    def _():
        start_rows(air_ref, slabs, row_sem, True)

    @pl.when(odd == 1)
    def _():
        start_rows(air_ref, slabs, row_sem, False)

    first = [
        pltpu.make_async_copy(border_ref, border, sem.at[0]),
        pltpu.make_async_copy(radiosity_ref, blocks_of, sem.at[1]),
    ]
    edge = [
        pltpu.make_async_copy(
            air_ref.at[:, x, pl.ds(y, LANES)], ends.at[i, j], end_sem.at[i, j]
        )
        for i, x in enumerate((0, depth - 1))
        for j, y in enumerate((0, width - LANES))
    ]
    for c in first + edge:
        c.start()
    spread[...] = jnp.zeros(spread.shape, F32)
    for c in first:
        c.wait()
    for s in range(blocks):
        own_ref[s] = blocks_of[:, s * LANES : (s + 1) * LANES]
    for s in range(borders):
        tile = own_ref[border[s]]
        near_out[at_small + s] = tile
        far_small[s] = tile
    for c in edge:
        c.wait()
    lane = iota((levels, LANES), 1)
    sub = iota((16, LANES), 0)
    corner = []
    for i in range(2):
        spread[i, pl.ds(0, levels, 2), :] = jnp.where(lane < LANES // 2, ends[i, 0], ends[i, 1])
        turned = spread[i].T
        tile = jnp.zeros((16, LANES), F32)
        for n, row in enumerate((turned[0:1], turned[LANES - 1 : LANES])):
            high = row.astype(BF16).astype(F32)
            tile = jnp.where(sub == 2 * n, high, tile)
            tile = jnp.where(sub == 2 * n + 1, row - high, tile)
        corner.append(tile)
    near_out[at_small + borders] = jnp.where(odd == 0, corner[1], corner[0]).astype(BF16)
    far_small[borders] = jnp.where(odd == 0, corner[0], corner[1]).astype(BF16)
    wait_rows(air_ref, slabs, row_sem)
    put_rows(slabs, near_out)


def pack(border_list, radiosity, air):
    levels, _, width = air.shape
    blocks = radiosity.shape[1] // LANES
    borders = border_list.shape[0]
    row_tiles = 2 * (width // LANES) * (levels // 16)
    tile = lambda n: jax.ShapeDtypeStruct((n, 16, LANES), BF16)
    return pl.pallas_call(
        pack_kernel,
        out_shape=(tile(row_tiles + borders + 1), tile(borders + 1), tile(blocks)),
        in_specs=[PLACE] * 3,
        out_specs=(WHOLE,) * 3,
        scratch_shapes=[
            SMEM(border_list.shape, border_list.dtype),
            VMEM(radiosity.shape, BF16),
            VMEM((2, 2, levels, LANES), F32),
            VMEM((2, LANES, LANES), F32),
            VMEM((2, levels, width), F32),
            DMA((2,)),
            DMA((2, 2)),
            DMA((2,)),
        ],
        compiler_params=params(8),
        cost_estimate=cost(PACK_COST),
        name="pack",
    )(in_hbm(border_list), in_hbm(radiosity), in_hbm(air))


def columns_kernel(air_ref, after_ref, columns):
    del after_ref
    levels, depth, width = air_ref.shape
    place = iota((depth, LANES), 1) // 2
    for j in range(2):
        packed = jnp.zeros((depth, LANES), F32)
        for z in range(levels):
            tile = air_ref[z, :, j * (width - LANES) : j * (width - LANES) + LANES]
            turn = (2 * z + 2 * j) % LANES
            packed = jnp.where(place == z, pltpu.roll(tile, turn, 1) if turn else tile, packed)
        for n, piece in enumerate(split(packed, 2)):
            columns[2 * j + n] = piece


def end_columns(air, after):
    return pl.pallas_call(
        columns_kernel,
        out_shape=jax.ShapeDtypeStruct((4, air.shape[1], LANES), BF16),
        in_specs=[WHOLE, PLACE],
        out_specs=WHOLE,
        compiler_params=params(8),
        cost_estimate=cost(COLUMNS_COST),
        name="columns",
    )(air, after)


def hold_kernel(value_ref, after_ref, out_ref):
    del after_ref
    out_ref[...] = value_ref[...]


def hold(value, after):
    return pl.pallas_call(
        hold_kernel,
        out_shape=jax.ShapeDtypeStruct(value.shape, value.dtype),
        in_specs=[WHOLE, PLACE],
        out_specs=WHOLE,
        compiler_params=params(8),
        cost_estimate=cost(HOLD_COST),
        name="hold",
    )(value, after)


def rows_kernel(air_ref, after_ref, out_ref, slabs, sem):
    del after_ref
    odd = lax.rem(lax.axis_index("district"), 2)

    @pl.when(odd == 1)
    def _():
        start_rows(air_ref, slabs, sem, True)

    @pl.when(odd == 0)
    def _():
        start_rows(air_ref, slabs, sem, False)

    wait_rows(air_ref, slabs, sem)
    put_rows(slabs, out_ref)


def rows(air, after):
    levels, _, width = air.shape
    count = 2 * (width // LANES) * (levels // 16)
    return pl.pallas_call(
        rows_kernel,
        out_shape=jax.ShapeDtypeStruct((count, 16, LANES), BF16),
        in_specs=[WHOLE, PLACE],
        out_specs=WHOLE,
        scratch_shapes=[VMEM((2, levels, width), F32), DMA((2,))],
        compiler_params=params(8),
        cost_estimate=cost(ROWS_COST),
        name="rows",
    )(air, after)


def join_kernel(own_ref, columns_ref, near_ref, far_ref, after_ref, out_ref):
    del after_ref
    odd = lax.rem(lax.axis_index("district"), 2)
    borders = far_ref.shape[0] - 1
    blocks = own_ref.shape[0]
    at_small = near_ref.shape[0] - far_ref.shape[0]
    for s in range(blocks):
        out_ref[s] = own_ref[s]
    for s in range(4):
        out_ref[blocks + 2 * borders + 2 + s] = columns_ref[s]
    for s in range(borders + 1):
        near, far = near_ref[at_small + s].astype(F32), far_ref[s].astype(F32)
        before = jnp.where(odd == 1, near, far).astype(BF16)
        after = jnp.where(odd == 1, far, near).astype(BF16)
        at = blocks + s if s < borders else blocks + 2 * borders
        out_ref[at] = before
        out_ref[at + (borders if s < borders else 1)] = after


def join(own, columns, near, far, after):
    count = own.shape[0] + columns.shape[0] + 2 * far.shape[0]
    return pl.pallas_call(
        join_kernel,
        out_shape=jax.ShapeDtypeStruct((count, 16, LANES), BF16),
        in_specs=[WHOLE] * 4 + [PLACE],
        out_specs=WHOLE,
        compiler_params=params(8),
        cost_estimate=cost(JOIN_COST),
        name="join",
    )(own, columns, near, far, after)


def stack_kernel(one_ref, two_ref, after_ref, out_ref):
    del after_ref
    part = one_ref.shape[0]
    for s in range(part):
        out_ref[s] = one_ref[s]
        out_ref[part + s] = two_ref[s]


def stack(one, two, after):
    return pl.pallas_call(
        stack_kernel,
        out_shape=jax.ShapeDtypeStruct((2 * one.shape[0], 16, LANES), BF16),
        in_specs=[WHOLE] * 2 + [PLACE],
        out_specs=WHOLE,
        compiler_params=params(8),
        cost_estimate=cost(JOIN_COST),
        name="stack",
    )(one, two, after)


def cell_masks(cell_ref, depth, width):
    patches = cell_ref.shape[0]
    cell = cell_ref[...].reshape(1, patches)
    x_of, y_of = cell // width, cell % width
    spots = iota((LANES, patches), 0)
    at_low = jnp.where(spots == y_of % LANES, 1.0, 0.0).astype(BF16)
    return at_low, spots == (y_of // LANES) * depth + x_of


def stencil_level(z, src, store, beyond):
    levels, depth, width = src.shape
    tiles = width // LANES
    half = depth // 2
    sub = iota((half, LANES), 0)
    lane = iota((half, LANES), 1)
    zero = jnp.zeros((half, LANES), F32)
    below, above = jnp.maximum(z - 1, 0), jnp.minimum(z + 1, levels - 1)
    under, over = flag(z > 0), flag(z < levels - 1)
    at = [slice(t * LANES, (t + 1) * LANES) for t in range(tiles)]
    at_x = [slice(x * half, (x + 1) * half) for x in range(2)]
    centre = [[src[z, i, j] for j in at] for i in at_x]
    for x in range(2):
        fore = [pltpu.roll(c, 1, 1) for c in centre[x]]
        back = [pltpu.roll(c, LANES - 1, 1) for c in centre[x]]
        for t in range(tiles):
            c = centre[x][t]
            before = pltpu.roll(centre[0][t], 1, 0) if x else beyond(0, t)
            after = beyond(1, t) if x else pltpu.roll(centre[1][t], half - 1, 0)
            total = src[below, at_x[x], at[t]] * under + src[above, at_x[x], at[t]] * over
            total = total + jnp.where(sub == 0, before, pltpu.roll(c, 1, 0))
            total = total + jnp.where(sub == half - 1, after, pltpu.roll(c, half - 1, 0))
            total = total + jnp.where(lane == 0, fore[t - 1] if t else zero, fore[t])
            total = total + jnp.where(
                lane == LANES - 1, back[t + 1] if t + 1 < tiles else zero, back[t]
            )
            store(x, t, total + CENTRE * c)


def first_kernel(air_ref, after_ref, once):
    del after_ref
    levels, depth, _ = air_ref.shape
    half = depth // 2
    zero = jnp.zeros((half, LANES), F32)

    def level(z, carry):
        def store(x, t, total):
            once[z, x * half : (x + 1) * half, t * LANES : (t + 1) * LANES] = total

        stencil_level(z, air_ref, store, lambda x, t: zero)
        return carry

    lax.fori_loop(0, levels, level, 0, unroll=levels // 2)


def first(air, after):
    return pl.pallas_call(
        first_kernel,
        out_shape=jax.ShapeDtypeStruct(air.shape, F32),
        in_specs=[WHOLE, PLACE],
        out_specs=WHOLE,
        compiler_params=params(12),
        cost_estimate=cost(FIRST_COST),
        name="first",
    )(air, after)


def second_kernel(
    air_ref,
    once,
    cell_ref,
    air_out,
    ground_out,
    sides_out,
    edge_out,
    cell_out,
    result,
    out_sem,
    edge_sem,
    *,
    spans,
):
    levels, depth, width = once.shape
    tiles = width // LANES
    half = depth // 2
    district = lax.axis_index("district")
    has_top, has_bottom = flag(district > 0), flag(district < lax.axis_size("district") - 1)
    at = [slice(t * LANES, (t + 1) * LANES) for t in range(tiles)]
    at_x = [slice(x * half, (x + 1) * half) for x in range(2)]

    def level(z, carry):
        def beyond(x, t):
            return air_ref[z, at_x[x], at[t]] * (has_bottom if x else has_top)

        def store(x, t, total):
            total = SQUARE * total
            result[z, at_x[x], at[t]] = total
            if t in (0, tiles - 1):
                sides_out[0 if t == 0 else 1, z, at_x[x]] = total

        stencil_level(z, once, store, beyond)
        return carry

    writes = []
    done = 0
    for k, count in enumerate(spans):
        lax.fori_loop(done, done + count, level, 0, unroll=count)
        span = pl.ds(done, count)
        done += count
        lanes = pl.ds(LANES, width - 2 * LANES)
        c = pltpu.make_async_copy(
            result.at[span, :, lanes], air_out.at[span, :, lanes], out_sem.at[k]
        )
        c.start()
        writes.append(c)
    for i, x in enumerate((0, 1, depth - 2, depth - 1)):
        c = pltpu.make_async_copy(result.at[:, x, lanes], edge_out.at[i], edge_sem.at[i])
        c.start()
        writes.append(c)
    ground_out[...] = result[0]
    at_low, at_high = cell_masks(cell_ref, depth, width)
    ground = jnp.concatenate([air_ref[0, :, j] for j in at], axis=0)
    picked = sum(
        jnp.dot(piece, at_low, preferred_element_type=F32) for piece in split(ground, 3)
    )
    cell_out[...] = jnp.sum(jnp.where(at_high, picked, 0.0), axis=0, keepdims=True)
    for c in writes:
        c.wait()


def second(air, once, cell):
    levels, depth, width = air.shape
    spans = (levels // 2, levels // 4, levels // 8, levels // 8)
    return pl.pallas_call(
        functools.partial(second_kernel, spans=spans),
        out_shape=(
            jax.ShapeDtypeStruct(air.shape, F32),
            jax.ShapeDtypeStruct((depth, width), F32),
            jax.ShapeDtypeStruct((2, levels, depth, LANES), F32),
            jax.ShapeDtypeStruct((4, levels, width - 2 * LANES), F32),
            jax.ShapeDtypeStruct((1, cell.shape[0]), F32),
        ),
        in_specs=[WHOLE] * 3,
        out_specs=(PLACE,) + (WHOLE,) * 4,
        scratch_shapes=[VMEM(air.shape, F32), DMA((len(spans),)), DMA((4,))],
        compiler_params=params(20),
        cost_estimate=cost(SECOND_COST),
        name="second",
    )(air, once, cell)


def main_kernel(
    cols_ref,
    weight_ref,
    mine_ref,
    theirs_ref,
    reflectance_ref,
    emissivity_ref,
    temp_ref,
    cell_ref,
    view_ref,
    air_cell_ref,
    ground_ref,
    sides_ref,
    next_ref,
    radiosity_out,
    surface_out,
    air_out,
    side_edge_out,
    source_out,
    ground_out,
    sides,
    pieces,
    out_sem,
):
    del next_ref
    levels, depth = sides_ref.shape[1:3]
    width = ground_ref.shape[1]
    tiles = width // LANES
    row_blocks, nonzero = view_ref.shape[0], view_ref.shape[1]
    blk = lax.axis_index("blk")
    blks = lax.axis_size("blk")
    has_left, has_right = flag(blk > 0), flag(blk < blks - 1)
    part = mine_ref.shape[0] // 2
    visible = part - 6
    for n, (ref, base) in enumerate(
        ((mine_ref, 0), (theirs_ref, 0), (mine_ref, part), (theirs_ref, part))
    ):
        for s in range(visible):
            pieces[n * visible + s] = ref[base + s]

    writes = []
    even = lax.rem(blk, 2) == 0

    def pair(ref, at):
        return ref[at].astype(F32) + ref[at + 1].astype(F32)

    def received(load):
        one, three = load(0), load(part)
        return jnp.where(even, three, one) * has_left, jnp.where(even, one, three) * has_right

    columns = [received(lambda base, n=n: pair(theirs_ref, base + visible + 2 + n)) for n in (0, 2)]
    corners = [received(lambda base, n=n: theirs_ref[base + visible + n].astype(F32)) for n in (0, 1)]
    sub = iota((depth, LANES), 0)
    lane = iota((depth, LANES), 1)
    half = depth // 2
    beside = []
    for side in range(2):
        k = 2 if side == 0 else 0
        shift = LANES - 1 if side == 0 else 0
        turn = lambda v: pltpu.roll(v, shift, 1) if shift else v
        near = turn(columns[1 - side][side])
        beyond = columns[1][0] if side == 0 else pltpu.roll(columns[0][1], LANES - 1, 1)
        own = pair(mine_ref, visible + 2 + 2 * side)
        own = own if side == 0 else pltpu.roll(own, LANES - 1, 1)
        top, bottom = (c[side][k : k + 1] + c[side][k + 1 : k + 2] for c in corners)
        around = jnp.where(sub == 0, top, pltpu.roll(near, 1, 0))
        around = around + jnp.where(sub == depth - 1, bottom, pltpu.roll(near, depth - 1, 0))
        around = around + jnp.where(lane < 2, 0.0, pltpu.roll(near, 2, 1))
        around = around + jnp.where(lane >= 2 * levels - 2, 0.0, pltpu.roll(near, LANES - 2, 1))
        outer = 2.0 * CENTRE * near + 2.0 * around + beyond + own * (has_right if side else has_left)
        if side == 0:
            value = jnp.where(lane % 2 == 0, outer, pltpu.roll(near, 1, 1))
        else:
            value = jnp.where(lane % 2 == 0, near, pltpu.roll(outer, 1, 1))
        beside.append(SQUARE * value)

    lane8 = iota((half, LANES), 1)
    both = [lane8 < 2, lane8 >= LANES - 2]

    for z in range(levels):
        for side in range(2):
            turn = (2 * LANES - 2 * z - 2 * side) % LANES
            for x in range(2):
                at = slice(x * half, (x + 1) * half)
                value = pltpu.roll(beside[side][at], turn, 1) if turn else beside[side][at]
                value = sides_ref[side, z, at] + jnp.where(both[side], value, 0.0)
                sides[side, z, at] = value
                for i, row in ((2, half - 2), (3, half - 1)) if x else ((0, 0), (1, 1)):
                    side_edge_out[side, i, z : z + 1] = value[row : row + 1]
    for side in range(2):
        lanes = pl.ds(side * (width - LANES), LANES)
        c = pltpu.make_async_copy(
            sides.at[side, pl.ds(1, levels - 1)],
            air_out.at[pl.ds(1, levels - 1), :, lanes],
            out_sem.at[side],
        )
        c.start()
        writes.append(c)
    blocks = []
    for r in range(row_blocks):
        picked = []
        for k in range(nonzero):
            c = cols_ref[r, k]
            owner = c // visible
            picked.append(pieces[jnp.bitwise_xor(owner, blk) * visible + (c - owner * visible)])
        blocks.append(
            lax.dot_general(
                jnp.concatenate(picked, axis=1),
                jnp.concatenate([view_ref[r, k] for k in range(nonzero)], axis=1),
                (((1,), (1,)), ((), ())),
                preferred_element_type=F32,
            )
        )
    irradiance = jnp.concatenate(blocks, axis=1)

    patches = cell_ref.shape[0]
    at_low, at_high = cell_masks(cell_ref, depth, width)
    air_cell = air_cell_ref[...]
    temp = temp_ref[...].reshape(1, patches)
    squared = temp * temp
    bands = reflectance_ref.shape[0]
    weight = jnp.zeros((bands, LANES), F32)
    for n in range(bands):
        weight = jnp.where(iota((bands, LANES), 0) == n, weight_ref[n], weight)
    weight = jnp.concatenate([weight] * (patches // LANES), axis=1)
    emission = weight * (emissivity_ref[...].reshape(1, patches) * (squared * squared))
    albedo = reflectance_ref[...].astype(F32)
    radiosity_out[...] = emission + albedo * irradiance
    absorbed = jnp.sum((1.0 - albedo) * irradiance, axis=0, keepdims=True)
    emitted = jnp.sum(emission, axis=0, keepdims=True)
    surface = temp + GAIN * (absorbed - emitted) - COUPLE * (temp - 1.0 - air_cell)
    surface_out[...] = surface
    flux = HEAT * (COUPLE * (surface - 1.0 - air_cell))
    source = sum(
        lax.dot_general(
            jnp.where(at_high, piece.astype(F32), 0.0).astype(BF16),
            at_low,
            (((1,), (1,)), ((), ())),
            preferred_element_type=F32,
        )
        for piece in split(flux, 3)
    )

    for t in range(tiles):
        at = slice(t * LANES, (t + 1) * LANES)
        here = source[t * depth : (t + 1) * depth]
        before = sides[0 if t == 0 else 1, 0] if t in (0, tiles - 1) else ground_ref[:, at]
        ground_out[:, at] = before + here
        for i, x in enumerate((0, 1, depth - 2, depth - 1)):
            source_out[i : i + 1, at] = here[x : x + 1]
    for c in writes:
        c.wait()


def main(
    cols, weight, mine, theirs, reflectance, emissivity, temp, cell, view, air_cell, ground, sides, following
):
    levels, depth = sides.shape[1:3]
    width = ground.shape[1]
    bands, patches = reflectance.shape
    visible = mine.shape[0] // 2 - 6
    return pl.pallas_call(
        main_kernel,
        out_shape=(
            jax.ShapeDtypeStruct((bands, patches), F32),
            jax.ShapeDtypeStruct((1, patches), F32),
            jax.ShapeDtypeStruct(following.shape, F32),
            jax.ShapeDtypeStruct((2, 4, levels, LANES), F32),
            jax.ShapeDtypeStruct((4, width), F32),
            jax.ShapeDtypeStruct((depth, width), F32),
        ),
        in_specs=[pl.BlockSpec(memory_space=SMEM)] * 2 + [WHOLE] * 10 + [PLACE],
        out_specs=(WHOLE, WHOLE, PLACE, WHOLE, WHOLE, WHOLE),
        scratch_shapes=[
            VMEM(sides.shape, F32),
            VMEM((4 * visible, 16, LANES), BF16),
            DMA((2,)),
        ],
        input_output_aliases={12: 2},
        compiler_params=params(20),
        cost_estimate=cost(MAIN_COST),
        name="main",
    )(
        cols,
        weight,
        mine,
        theirs,
        reflectance,
        emissivity,
        temp,
        cell,
        view,
        air_cell,
        ground,
        sides,
        in_hbm(following),
    )


def finish_kernel(
    air_ref,
    edge_ref,
    side_ref,
    source_ref,
    ground_ref,
    radiosity_ref,
    surface_ref,
    near_ref,
    far_ref,
    out_ref,
    radiosity_out,
    surface_out,
    slabs,
    sem,
    value_sem,
):
    del air_ref
    levels, depth, width = out_ref.shape
    parts = levels // 16
    tiles = width // LANES
    odd = lax.rem(lax.axis_index("district"), 2)
    ground = iota((levels, LANES), 0) == 0
    copies = [
        pltpu.make_async_copy(ground_ref.at[x], out_ref.at[0, x], sem.at[2 + x])
        for x in range(2, depth - 2)
    ]
    copies += [
        pltpu.make_async_copy(radiosity_ref, radiosity_out, value_sem.at[0]),
        pltpu.make_async_copy(surface_ref.at[0], surface_out, value_sem.at[1]),
    ]
    for c in copies:
        c.start()
    for side in range(2):
        use_near = (odd == 1) if side == 0 else (odd == 0)

        def received(k, i):
            at = [(k * tiles + i) * parts + q for q in range(parts)]
            near, far = (jnp.concatenate([ref[n] for n in at]) for ref in (near_ref, far_ref))
            return jnp.where(use_near, near.astype(F32), far.astype(F32))

        def base(n, i):
            if i in (0, tiles - 1):
                value = side_ref[0 if i == 0 else 1, n]
            else:
                value = edge_ref[n, :, (i - 1) * LANES : i * LANES]
            return value + jnp.where(ground, source_ref[n : n + 1, i * LANES : (i + 1) * LANES], 0.0)

        outer, inner = (0, 1) if side == 0 else (3, 2)
        for i, (c, around) in enumerate(plane_neighbours(functools.partial(received, 0), tiles)):
            at = slice(i * LANES, (i + 1) * LANES)
            reach = (2.0 * CENTRE) * c + 2.0 * around + received(1, i)
            slabs[outer, :, at] = base(outer, i) + SQUARE * reach
            slabs[inner, :, at] = base(inner, i) + SQUARE * c
        for i in (outer, inner):
            x = (0, 1, depth - 2, depth - 1)[i]
            c = pltpu.make_async_copy(slabs.at[i], out_ref.at[:, x, :], sem.at[i])
            c.start()
            copies.append(c)
    for c in copies:
        c.wait()


def finish(air, edge, side, source, ground, radiosity, surface, near, far):
    levels, depth, width = air.shape
    return pl.pallas_call(
        finish_kernel,
        out_shape=(
            jax.ShapeDtypeStruct(air.shape, F32),
            jax.ShapeDtypeStruct(radiosity.shape, F32),
            jax.ShapeDtypeStruct(surface.shape[1:], F32),
        ),
        in_specs=[PLACE] + [WHOLE] * 8,
        out_specs=(PLACE,) * 3,
        scratch_shapes=[VMEM((4, levels, width), F32), DMA((depth,)), DMA((2,))],
        input_output_aliases={0: 0},
        compiler_params=params(8),
        name="finish",
    )(in_hbm(air), edge, side, source, ground, radiosity, surface, near, far)


def swap(value, axis, pairs):
    return lax.ppermute(value, axis, [p for a, b in pairs for p in ((a, b), (b, a))])


def body(
    view_factor,
    view_cols,
    border_list,
    radiosity,
    reflectance,
    emissivity,
    band_weight,
    surface_temp,
    patch_cell,
    air,
):
    districts, blks = lax.axis_size("district"), lax.axis_size("blk")
    near_pairs = [(i, i + 1) for i in range(0, districts - 1, 2)]
    far_pairs = [(i, i + 1) for i in range(1, districts - 1, 2)]
    near, far_small, own = pack(border_list, radiosity, air)
    near = swap(near, "district", near_pairs)
    far_small = swap(hold(far_small, own), "district", far_pairs)
    columns = end_columns(air, own)
    once = first(air, columns)
    following, ground, sides, edge, air_cell = second(air, once, patch_cell)
    far = rows(air, once)
    own = join(own, columns, near, far_small, far)
    far = hold(far, own)
    across = swap(own, "blk", [(i, i ^ 2) for i in range(blks) if i < i ^ 2])
    mine = stack(own, across, far)
    far = swap(far, "district", far_pairs)
    theirs = swap(mine, "blk", [(i, i ^ 1) for i in range(blks) if i < i ^ 1])
    radiosity, surface, air_next, side, source, ground = main(
        view_cols,
        band_weight,
        mine,
        theirs,
        reflectance,
        emissivity,
        surface_temp,
        patch_cell,
        view_factor,
        air_cell,
        ground,
        sides,
        following,
    )
    air_next, radiosity_next, surface_next = finish(
        air_next, edge, side, source, ground, radiosity, surface, near, far
    )
    return radiosity_next, surface_next, air_next


def solution(mesh):
    in_specs = (
        P(("district", "blk"), None, None, None),
        P(("district", "blk"), None),
        P(("district", "blk")),
        P(None, ("district", "blk")),
        P(None, ("district", "blk")),
        P(("district", "blk")),
        P(),
        P(("district", "blk")),
        P(("district", "blk")),
        P(None, "district", "blk"),
    )
    out_specs = (P(None, ("district", "blk")), P(("district", "blk")), P(None, "district", "blk"))
    return jax.shard_map(body, mesh=mesh, in_specs=in_specs, out_specs=out_specs, check_vma=False)
```

```python
import functools

import jax
import jax.numpy as jnp
from jax import lax
from jax.experimental import pallas as pl
from jax.experimental.pallas import tpu as pltpu
from jax.sharding import PartitionSpec as P

KAPPA = 0.15
GAIN = 0.02
COUPLE = 0.2
HEAT = 1.0
CENTRE = (1.0 - 6.0 * KAPPA) / KAPPA
SQUARE = KAPPA * KAPPA

F32 = jnp.float32
BF16 = jnp.bfloat16
LANES = 128
VMEM = pltpu.VMEM
SMEM = pltpu.SMEM
DMA = pltpu.SemaphoreType.DMA
PACK_COST, COLUMNS_COST, ROWS_COST, JOIN_COST, HOLD_COST, FIRST_COST, SECOND_COST, MAIN_COST = 2, 0.1, 1, 1, 0.1, 1, 1, 1


def params(mebibytes):
    return pltpu.CompilerParams(vmem_limit_bytes=mebibytes << 20)


def cost(microseconds):
    return pl.CostEstimate(flops=int(microseconds * 1_000_000_000), bytes_accessed=0, transcendentals=0)


def in_hbm(value):
    return pltpu.with_memory_space_constraint(value, pltpu.HBM)


WHOLE = pl.BlockSpec(memory_space=VMEM)
PLACE = pl.BlockSpec(memory_space=pl.ANY)


def iota(shape, axis):
    return lax.broadcasted_iota(jnp.int32, shape, axis)


def flag(condition):
    return jnp.where(condition, 1.0, 0.0).astype(F32)


def split(value, pieces):
    out = []
    for _ in range(pieces):
        piece = value.astype(BF16)
        out.append(piece)
        value = value - piece.astype(F32)
    return out


def plane_neighbours(load, tiles):
    centre = [load(i) for i in range(tiles)]
    rows = centre[0].shape[0]
    lane = iota((rows, LANES), 1)
    row = iota((rows, LANES), 0)
    right = [pltpu.roll(c, 1, 1) for c in centre]
    left = [pltpu.roll(c, LANES - 1, 1) for c in centre]
    zero = jnp.zeros((rows, LANES), F32)
    for i, c in enumerate(centre):
        total = jnp.where(lane == 0, right[i - 1] if i else zero, right[i])
        total = total + jnp.where(
            lane == LANES - 1, left[i + 1] if i + 1 < tiles else zero, left[i]
        )
        total = total + jnp.where(row == 0, 0.0, pltpu.roll(c, 1, 0))
        total = total + jnp.where(row == rows - 1, 0.0, pltpu.roll(c, rows - 1, 0))
        yield c, total


def start_rows(air_ref, slabs, sem, last):
    depth = air_ref.shape[1]
    for i, r in enumerate((depth - 1, depth - 2) if last else (0, 1)):
        pltpu.make_async_copy(air_ref.at[:, r, :], slabs.at[i], sem.at[i]).start()


def wait_rows(air_ref, slabs, sem):
    for i in range(2):
        pltpu.make_async_copy(air_ref.at[:, i, :], slabs.at[i], sem.at[i]).wait()


def put_rows(slabs, out_ref):
    levels, width = slabs.shape[1:]
    tiles, parts = width // LANES, levels // 16

    def lost(i):
        value = slabs[0, :, i * LANES : (i + 1) * LANES]
        return value - value.astype(BF16).astype(F32)

    for i, (c, around) in enumerate(plane_neighbours(lost, tiles)):
        at = slice(i * LANES, (i + 1) * LANES)
        values = slabs[0, :, at], slabs[1, :, at] + CENTRE * 2.0 * c + 2.0 * around
        for k, value in enumerate(values):
            value = value.astype(BF16)
            for q in range(parts):
                out_ref[(k * tiles + i) * parts + q] = value[16 * q : 16 * q + 16]


def pack_kernel(
    border_ref,
    radiosity_ref,
    air_ref,
    near_out,
    far_small,
    own_ref,
    slabs,
    border,
    blocks_of,
    ends,
    spread,
    sem,
    end_sem,
    row_sem,
):
    levels, depth, width = air_ref.shape
    blocks = radiosity_ref.shape[1] // LANES
    borders = border_ref.shape[0]
    at_small = near_out.shape[0] - far_small.shape[0]
    odd = lax.rem(lax.axis_index("district"), 2)

    @pl.when(odd == 0)
    def _():
        start_rows(air_ref, slabs, row_sem, True)

    @pl.when(odd == 1)
    def _():
        start_rows(air_ref, slabs, row_sem, False)

    first = [
        pltpu.make_async_copy(border_ref, border, sem.at[0]),
        pltpu.make_async_copy(radiosity_ref, blocks_of, sem.at[1]),
    ]
    edge = [
        pltpu.make_async_copy(
            air_ref.at[:, x, pl.ds(y, LANES)], ends.at[i, j], end_sem.at[i, j]
        )
        for i, x in enumerate((0, depth - 1))
        for j, y in enumerate((0, width - LANES))
    ]
    for c in first + edge:
        c.start()
    spread[...] = jnp.zeros(spread.shape, F32)
    for c in first:
        c.wait()
    for s in range(blocks):
        own_ref[s] = blocks_of[:, s * LANES : (s + 1) * LANES]
    for s in range(borders):
        tile = own_ref[border[s]]
        near_out[at_small + s] = tile
        far_small[s] = tile
    for c in edge:
        c.wait()
    lane = iota((levels, LANES), 1)
    sub = iota((16, LANES), 0)
    corner = []
    for i in range(2):
        spread[i, pl.ds(0, levels, 2), :] = jnp.where(lane < LANES // 2, ends[i, 0], ends[i, 1])
        turned = spread[i].T
        tile = jnp.zeros((16, LANES), F32)
        for n, row in enumerate((turned[0:1], turned[LANES - 1 : LANES])):
            high = row.astype(BF16).astype(F32)
            tile = jnp.where(sub == 2 * n, high, tile)
            tile = jnp.where(sub == 2 * n + 1, row - high, tile)
        corner.append(tile)
    near_out[at_small + borders] = jnp.where(odd == 0, corner[1], corner[0]).astype(BF16)
    far_small[borders] = jnp.where(odd == 0, corner[0], corner[1]).astype(BF16)
    wait_rows(air_ref, slabs, row_sem)
    put_rows(slabs, near_out)


def pack(border_list, radiosity, air):
    levels, _, width = air.shape
    blocks = radiosity.shape[1] // LANES
    borders = border_list.shape[0]
    row_tiles = 2 * (width // LANES) * (levels // 16)
    tile = lambda n: jax.ShapeDtypeStruct((n, 16, LANES), BF16)
    return pl.pallas_call(
        pack_kernel,
        out_shape=(
            tile(row_tiles + borders + 1),
            tile(borders + 1),
            tile(blocks),
            jax.ShapeDtypeStruct((2, levels, width), F32),
        ),
        in_specs=[PLACE] * 3,
        out_specs=(WHOLE,) * 4,
        scratch_shapes=[
            SMEM(border_list.shape, border_list.dtype),
            VMEM(radiosity.shape, BF16),
            VMEM((2, 2, levels, LANES), F32),
            VMEM((2, LANES, LANES), F32),
            DMA((2,)),
            DMA((2, 2)),
            DMA((2,)),
        ],
        compiler_params=params(8),
        cost_estimate=cost(PACK_COST),
        name="pack",
    )(in_hbm(border_list), in_hbm(radiosity), in_hbm(air))


def columns_kernel(air_ref, after_ref, columns):
    del after_ref
    levels, depth, width = air_ref.shape
    place = iota((depth, LANES), 1) // 2
    for j in range(2):
        packed = jnp.zeros((depth, LANES), F32)
        for z in range(levels):
            tile = air_ref[z, :, j * (width - LANES) : j * (width - LANES) + LANES]
            turn = (2 * z + 2 * j) % LANES
            packed = jnp.where(place == z, pltpu.roll(tile, turn, 1) if turn else tile, packed)
        for n, piece in enumerate(split(packed, 2)):
            columns[2 * j + n] = piece


def end_columns(air, after):
    return pl.pallas_call(
        columns_kernel,
        out_shape=jax.ShapeDtypeStruct((4, air.shape[1], LANES), BF16),
        in_specs=[WHOLE, PLACE],
        out_specs=WHOLE,
        compiler_params=params(8),
        cost_estimate=cost(COLUMNS_COST),
        name="columns",
    )(air, after)


def hold_kernel(value_ref, after_ref, out_ref):
    del after_ref
    out_ref[...] = value_ref[...]


def hold(value, after):
    return pl.pallas_call(
        hold_kernel,
        out_shape=jax.ShapeDtypeStruct(value.shape, value.dtype),
        in_specs=[WHOLE, PLACE],
        out_specs=WHOLE,
        compiler_params=params(8),
        cost_estimate=cost(HOLD_COST),
        name="hold",
    )(value, after)


def rows_kernel(air_ref, after_ref, out_ref, slabs, sem):
    del after_ref
    odd = lax.rem(lax.axis_index("district"), 2)

    @pl.when(odd == 1)
    def _():
        start_rows(air_ref, slabs, sem, True)

    @pl.when(odd == 0)
    def _():
        start_rows(air_ref, slabs, sem, False)

    wait_rows(air_ref, slabs, sem)
    put_rows(slabs, out_ref)


def rows(air, after):
    levels, _, width = air.shape
    count = 2 * (width // LANES) * (levels // 16)
    return pl.pallas_call(
        rows_kernel,
        out_shape=(
            jax.ShapeDtypeStruct((count, 16, LANES), BF16),
            jax.ShapeDtypeStruct((2, levels, width), F32),
        ),
        in_specs=[WHOLE, PLACE],
        out_specs=(WHOLE, WHOLE),
        scratch_shapes=[DMA((2,))],
        compiler_params=params(8),
        cost_estimate=cost(ROWS_COST),
        name="rows",
    )(air, after)


def join_kernel(own_ref, columns_ref, near_ref, far_ref, after_ref, out_ref):
    del after_ref
    odd = lax.rem(lax.axis_index("district"), 2)
    borders = far_ref.shape[0] - 1
    blocks = own_ref.shape[0]
    at_small = near_ref.shape[0] - far_ref.shape[0]
    for s in range(blocks):
        out_ref[s] = own_ref[s]
    for s in range(4):
        out_ref[blocks + 2 * borders + 2 + s] = columns_ref[s]
    for s in range(borders + 1):
        near, far = near_ref[at_small + s].astype(F32), far_ref[s].astype(F32)
        before = jnp.where(odd == 1, near, far).astype(BF16)
        after = jnp.where(odd == 1, far, near).astype(BF16)
        at = blocks + s if s < borders else blocks + 2 * borders
        out_ref[at] = before
        out_ref[at + (borders if s < borders else 1)] = after


def join(own, columns, near, far, after):
    count = own.shape[0] + columns.shape[0] + 2 * far.shape[0]
    return pl.pallas_call(
        join_kernel,
        out_shape=jax.ShapeDtypeStruct((count, 16, LANES), BF16),
        in_specs=[WHOLE] * 4 + [PLACE],
        out_specs=WHOLE,
        compiler_params=params(8),
        cost_estimate=cost(JOIN_COST),
        name="join",
    )(own, columns, near, far, after)


def stack_kernel(one_ref, two_ref, after_ref, out_ref):
    del after_ref
    part = one_ref.shape[0]
    for s in range(part):
        out_ref[s] = one_ref[s]
        out_ref[part + s] = two_ref[s]


def stack(one, two, after):
    return pl.pallas_call(
        stack_kernel,
        out_shape=jax.ShapeDtypeStruct((2 * one.shape[0], 16, LANES), BF16),
        in_specs=[WHOLE] * 2 + [PLACE],
        out_specs=WHOLE,
        compiler_params=params(8),
        cost_estimate=cost(JOIN_COST),
        name="stack",
    )(one, two, after)


def cell_masks(cell_ref, depth, width):
    patches = cell_ref.shape[0]
    cell = cell_ref[...].reshape(1, patches)
    x_of, y_of = cell // width, cell % width
    spots = iota((LANES, patches), 0)
    at_low = jnp.where(spots == y_of % LANES, 1.0, 0.0).astype(BF16)
    return at_low, spots == (y_of // LANES) * depth + x_of


def stencil_level(z, src, store):
    levels, depth, width = src.shape
    tiles = width // LANES
    half = depth // 2
    sub = iota((half, LANES), 0)
    lane = iota((half, LANES), 1)
    zero = jnp.zeros((half, LANES), F32)
    below, above = jnp.maximum(z - 1, 0), jnp.minimum(z + 1, levels - 1)
    under, over = flag(z > 0), flag(z < levels - 1)
    at = [slice(t * LANES, (t + 1) * LANES) for t in range(tiles)]
    at_x = [slice(x * half, (x + 1) * half) for x in range(2)]
    centre = [[src[z, i, j] for j in at] for i in at_x]
    for x in range(2):
        fore = [pltpu.roll(c, 1, 1) for c in centre[x]]
        back = [pltpu.roll(c, LANES - 1, 1) for c in centre[x]]
        for t in range(tiles):
            c = centre[x][t]
            before = pltpu.roll(centre[0][t], 1, 0) if x else zero
            after = zero if x else pltpu.roll(centre[1][t], half - 1, 0)
            total = src[below, at_x[x], at[t]] * under + src[above, at_x[x], at[t]] * over
            total = total + jnp.where(sub == 0, before, pltpu.roll(c, 1, 0))
            total = total + jnp.where(sub == half - 1, after, pltpu.roll(c, half - 1, 0))
            total = total + jnp.where(lane == 0, fore[t - 1] if t else zero, fore[t])
            total = total + jnp.where(
                lane == LANES - 1, back[t + 1] if t + 1 < tiles else zero, back[t]
            )
            store(x, t, total + CENTRE * c)


def first_kernel(air_ref, after_ref, once):
    del after_ref
    levels, depth, _ = air_ref.shape
    half = depth // 2

    def level(z, carry):
        def store(x, t, total):
            once[z, x * half : (x + 1) * half, t * LANES : (t + 1) * LANES] = total

        stencil_level(z, air_ref, store)
        return carry

    lax.fori_loop(0, levels, level, 0, unroll=levels // 2)


def first(air, after):
    return pl.pallas_call(
        first_kernel,
        out_shape=jax.ShapeDtypeStruct(air.shape, F32),
        in_specs=[WHOLE, PLACE],
        out_specs=WHOLE,
        compiler_params=params(12),
        cost_estimate=cost(FIRST_COST),
        name="first",
    )(air, after)


def second_kernel(
    air_ref,
    once,
    cell_ref,
    air_out,
    ground_out,
    sides_out,
    edge_out,
    cell_out,
    result,
    out_sem,
    edge_sem,
    *,
    spans,
):
    levels, depth, width = once.shape
    tiles = width // LANES
    half = depth // 2
    at = [slice(t * LANES, (t + 1) * LANES) for t in range(tiles)]
    at_x = [slice(x * half, (x + 1) * half) for x in range(2)]

    def level(z, carry):
        def store(x, t, total):
            total = SQUARE * total
            result[z, at_x[x], at[t]] = total
            if t in (0, tiles - 1):
                sides_out[0 if t == 0 else 1, z, at_x[x]] = total

        stencil_level(z, once, store)
        return carry

    writes = []
    done = 0
    for k, count in enumerate(spans):
        lax.fori_loop(done, done + count, level, 0, unroll=count)
        span = pl.ds(done, count)
        done += count
        lanes = pl.ds(LANES, width - 2 * LANES)
        c = pltpu.make_async_copy(
            result.at[span, :, lanes], air_out.at[span, :, lanes], out_sem.at[k]
        )
        c.start()
        writes.append(c)
    for i, x in enumerate((0, 1, depth - 2, depth - 1)):
        c = pltpu.make_async_copy(result.at[:, x, lanes], edge_out.at[i], edge_sem.at[i])
        c.start()
        writes.append(c)
    ground_out[...] = result[0]
    at_low, at_high = cell_masks(cell_ref, depth, width)
    ground = jnp.concatenate([air_ref[0, :, j] for j in at], axis=0)
    picked = sum(
        jnp.dot(piece, at_low, preferred_element_type=F32) for piece in split(ground, 3)
    )
    cell_out[...] = jnp.sum(jnp.where(at_high, picked, 0.0), axis=0, keepdims=True)
    for c in writes:
        c.wait()


def second(air, once, cell):
    levels, depth, width = air.shape
    spans = (levels // 2, levels // 4, levels // 8, levels // 8)
    return pl.pallas_call(
        functools.partial(second_kernel, spans=spans),
        out_shape=(
            jax.ShapeDtypeStruct(air.shape, F32),
            jax.ShapeDtypeStruct((depth, width), F32),
            jax.ShapeDtypeStruct((2, levels, depth, LANES), F32),
            jax.ShapeDtypeStruct((4, levels, width - 2 * LANES), F32),
            jax.ShapeDtypeStruct((1, cell.shape[0]), F32),
        ),
        in_specs=[WHOLE] * 3,
        out_specs=(PLACE,) + (WHOLE,) * 4,
        scratch_shapes=[VMEM(air.shape, F32), DMA((len(spans),)), DMA((4,))],
        compiler_params=params(20),
        cost_estimate=cost(SECOND_COST),
        name="second",
    )(air, once, cell)


def main_kernel(
    cols_ref,
    weight_ref,
    mine_ref,
    theirs_ref,
    reflectance_ref,
    emissivity_ref,
    temp_ref,
    cell_ref,
    view_ref,
    air_cell_ref,
    ground_ref,
    sides_ref,
    next_ref,
    radiosity_out,
    surface_out,
    air_out,
    side_edge_out,
    source_out,
    ground_out,
    sides,
    pieces,
    out_sem,
):
    del next_ref
    levels, depth = sides_ref.shape[1:3]
    width = ground_ref.shape[1]
    tiles = width // LANES
    row_blocks, nonzero = view_ref.shape[0], view_ref.shape[1]
    blk = lax.axis_index("blk")
    blks = lax.axis_size("blk")
    has_left, has_right = flag(blk > 0), flag(blk < blks - 1)
    part = mine_ref.shape[0] // 2
    visible = part - 6
    for n, (ref, base) in enumerate(
        ((mine_ref, 0), (theirs_ref, 0), (mine_ref, part), (theirs_ref, part))
    ):
        for s in range(visible):
            pieces[n * visible + s] = ref[base + s]

    writes = []
    even = lax.rem(blk, 2) == 0

    def pair(ref, at):
        return ref[at].astype(F32) + ref[at + 1].astype(F32)

    def received(load):
        one, three = load(0), load(part)
        return jnp.where(even, three, one) * has_left, jnp.where(even, one, three) * has_right

    columns = [received(lambda base, n=n: pair(theirs_ref, base + visible + 2 + n)) for n in (0, 2)]
    corners = [received(lambda base, n=n: theirs_ref[base + visible + n].astype(F32)) for n in (0, 1)]
    sub = iota((depth, LANES), 0)
    lane = iota((depth, LANES), 1)
    half = depth // 2
    beside = []
    for side in range(2):
        k = 2 if side == 0 else 0
        shift = LANES - 1 if side == 0 else 0
        turn = lambda v: pltpu.roll(v, shift, 1) if shift else v
        near = turn(columns[1 - side][side])
        beyond = columns[1][0] if side == 0 else pltpu.roll(columns[0][1], LANES - 1, 1)
        own = pair(mine_ref, visible + 2 + 2 * side)
        own = own if side == 0 else pltpu.roll(own, LANES - 1, 1)
        top, bottom = (c[side][k : k + 1] + c[side][k + 1 : k + 2] for c in corners)
        around = jnp.where(sub == 0, top, pltpu.roll(near, 1, 0))
        around = around + jnp.where(sub == depth - 1, bottom, pltpu.roll(near, depth - 1, 0))
        around = around + jnp.where(lane < 2, 0.0, pltpu.roll(near, 2, 1))
        around = around + jnp.where(lane >= 2 * levels - 2, 0.0, pltpu.roll(near, LANES - 2, 1))
        outer = 2.0 * CENTRE * near + 2.0 * around + beyond + own * (has_right if side else has_left)
        if side == 0:
            value = jnp.where(lane % 2 == 0, outer, pltpu.roll(near, 1, 1))
        else:
            value = jnp.where(lane % 2 == 0, near, pltpu.roll(outer, 1, 1))
        beside.append(SQUARE * value)

    lane8 = iota((half, LANES), 1)
    both = [lane8 < 2, lane8 >= LANES - 2]

    for z in range(levels):
        for side in range(2):
            turn = (2 * LANES - 2 * z - 2 * side) % LANES
            for x in range(2):
                at = slice(x * half, (x + 1) * half)
                value = pltpu.roll(beside[side][at], turn, 1) if turn else beside[side][at]
                value = sides_ref[side, z, at] + jnp.where(both[side], value, 0.0)
                sides[side, z, at] = value
                for i, row in ((2, half - 2), (3, half - 1)) if x else ((0, 0), (1, 1)):
                    side_edge_out[side, i, z : z + 1] = value[row : row + 1]
    for side in range(2):
        lanes = pl.ds(side * (width - LANES), LANES)
        c = pltpu.make_async_copy(
            sides.at[side, pl.ds(1, levels - 1)],
            air_out.at[pl.ds(1, levels - 1), :, lanes],
            out_sem.at[side],
        )
        c.start()
        writes.append(c)
    blocks = []
    for r in range(row_blocks):
        picked = []
        for k in range(nonzero):
            c = cols_ref[r, k]
            owner = c // visible
            picked.append(pieces[jnp.bitwise_xor(owner, blk) * visible + (c - owner * visible)])
        blocks.append(
            lax.dot_general(
                jnp.concatenate(picked, axis=1),
                jnp.concatenate([view_ref[r, k] for k in range(nonzero)], axis=1),
                (((1,), (1,)), ((), ())),
                preferred_element_type=F32,
            )
        )
    irradiance = jnp.concatenate(blocks, axis=1)

    patches = cell_ref.shape[0]
    at_low, at_high = cell_masks(cell_ref, depth, width)
    air_cell = air_cell_ref[...]
    temp = temp_ref[...].reshape(1, patches)
    squared = temp * temp
    bands = reflectance_ref.shape[0]
    weight = jnp.zeros((bands, LANES), F32)
    for n in range(bands):
        weight = jnp.where(iota((bands, LANES), 0) == n, weight_ref[n], weight)
    weight = jnp.concatenate([weight] * (patches // LANES), axis=1)
    emission = weight * (emissivity_ref[...].reshape(1, patches) * (squared * squared))
    albedo = reflectance_ref[...].astype(F32)
    radiosity_out[...] = emission + albedo * irradiance
    absorbed = jnp.sum((1.0 - albedo) * irradiance, axis=0, keepdims=True)
    emitted = jnp.sum(emission, axis=0, keepdims=True)
    surface = temp + GAIN * (absorbed - emitted) - COUPLE * (temp - 1.0 - air_cell)
    surface_out[...] = surface
    flux = HEAT * (COUPLE * (surface - 1.0 - air_cell))
    source = sum(
        lax.dot_general(
            jnp.where(at_high, piece.astype(F32), 0.0).astype(BF16),
            at_low,
            (((1,), (1,)), ((), ())),
            preferred_element_type=F32,
        )
        for piece in split(flux, 3)
    )

    for t in range(tiles):
        at = slice(t * LANES, (t + 1) * LANES)
        here = source[t * depth : (t + 1) * depth]
        before = sides[0 if t == 0 else 1, 0] if t in (0, tiles - 1) else ground_ref[:, at]
        ground_out[:, at] = before + here
        for i, x in enumerate((0, 1, depth - 2, depth - 1)):
            source_out[i : i + 1, at] = here[x : x + 1]
    for c in writes:
        c.wait()


def main(
    cols, weight, mine, theirs, reflectance, emissivity, temp, cell, view, air_cell, ground, sides, following
):
    levels, depth = sides.shape[1:3]
    width = ground.shape[1]
    bands, patches = reflectance.shape
    visible = mine.shape[0] // 2 - 6
    return pl.pallas_call(
        main_kernel,
        out_shape=(
            jax.ShapeDtypeStruct((bands, patches), F32),
            jax.ShapeDtypeStruct((1, patches), F32),
            jax.ShapeDtypeStruct(following.shape, F32),
            jax.ShapeDtypeStruct((2, 4, levels, LANES), F32),
            jax.ShapeDtypeStruct((4, width), F32),
            jax.ShapeDtypeStruct((depth, width), F32),
        ),
        in_specs=[pl.BlockSpec(memory_space=SMEM)] * 2 + [WHOLE] * 10 + [PLACE],
        out_specs=(WHOLE, WHOLE, PLACE, WHOLE, WHOLE, WHOLE),
        scratch_shapes=[
            VMEM(sides.shape, F32),
            VMEM((4 * visible, 16, LANES), BF16),
            DMA((2,)),
        ],
        input_output_aliases={12: 2},
        compiler_params=params(20),
        cost_estimate=cost(MAIN_COST),
        name="main",
    )(
        cols,
        weight,
        mine,
        theirs,
        reflectance,
        emissivity,
        temp,
        cell,
        view,
        air_cell,
        ground,
        sides,
        in_hbm(following),
    )


def finish_kernel(
    air_ref,
    edge_ref,
    side_ref,
    source_ref,
    ground_ref,
    radiosity_ref,
    surface_ref,
    near_ref,
    far_ref,
    near_own,
    far_own,
    out_ref,
    radiosity_out,
    surface_out,
    slabs,
    sem,
    value_sem,
):
    del air_ref
    levels, depth, width = out_ref.shape
    parts = levels // 16
    tiles = width // LANES
    district = lax.axis_index("district")
    odd = lax.rem(district, 2)
    has = flag(district > 0), flag(district < lax.axis_size("district") - 1)
    ground = iota((levels, LANES), 0) == 0
    copies = [
        pltpu.make_async_copy(ground_ref.at[x], out_ref.at[0, x], sem.at[2 + x])
        for x in range(2, depth - 2)
    ]
    copies += [
        pltpu.make_async_copy(radiosity_ref, radiosity_out, value_sem.at[0]),
        pltpu.make_async_copy(surface_ref.at[0], surface_out, value_sem.at[1]),
    ]
    for c in copies:
        c.start()
    for side in range(2):
        use_near = (odd == 1) if side == 0 else (odd == 0)

        def received(k, i):
            at = [(k * tiles + i) * parts + q for q in range(parts)]
            near, far = (jnp.concatenate([ref[n] for n in at]) for ref in (near_ref, far_ref))
            return jnp.where(use_near, near.astype(F32), far.astype(F32))

        def base(n, i):
            if i in (0, tiles - 1):
                value = side_ref[0 if i == 0 else 1, n]
            else:
                value = edge_ref[n, :, (i - 1) * LANES : i * LANES]
            return value + jnp.where(ground, source_ref[n : n + 1, i * LANES : (i + 1) * LANES], 0.0)

        outer, inner = (0, 1) if side == 0 else (3, 2)
        for i, (c, around) in enumerate(plane_neighbours(functools.partial(received, 0), tiles)):
            at = slice(i * LANES, (i + 1) * LANES)
            own = jnp.where(use_near, near_own[0, :, at], far_own[0, :, at]) * has[side]
            reach = (2.0 * CENTRE) * c + 2.0 * around + received(1, i) + own
            slabs[outer, :, at] = base(outer, i) + SQUARE * reach
            slabs[inner, :, at] = base(inner, i) + SQUARE * c
        for i in (outer, inner):
            x = (0, 1, depth - 2, depth - 1)[i]
            c = pltpu.make_async_copy(slabs.at[i], out_ref.at[:, x, :], sem.at[i])
            c.start()
            copies.append(c)
    for c in copies:
        c.wait()


def finish(air, edge, side, source, ground, radiosity, surface, near, far, near_own, far_own):
    levels, depth, width = air.shape
    return pl.pallas_call(
        finish_kernel,
        out_shape=(
            jax.ShapeDtypeStruct(air.shape, F32),
            jax.ShapeDtypeStruct(radiosity.shape, F32),
            jax.ShapeDtypeStruct(surface.shape[1:], F32),
        ),
        in_specs=[PLACE] + [WHOLE] * 10,
        out_specs=(PLACE,) * 3,
        scratch_shapes=[VMEM((4, levels, width), F32), DMA((depth,)), DMA((2,))],
        input_output_aliases={0: 0},
        compiler_params=params(8),
        name="finish",
    )(in_hbm(air), edge, side, source, ground, radiosity, surface, near, far, near_own, far_own)


def swap(value, axis, pairs):
    return lax.ppermute(value, axis, [p for a, b in pairs for p in ((a, b), (b, a))])


def body(
    view_factor,
    view_cols,
    border_list,
    radiosity,
    reflectance,
    emissivity,
    band_weight,
    surface_temp,
    patch_cell,
    air,
):
    districts, blks = lax.axis_size("district"), lax.axis_size("blk")
    near_pairs = [(i, i + 1) for i in range(0, districts - 1, 2)]
    far_pairs = [(i, i + 1) for i in range(1, districts - 1, 2)]
    near, far_small, own, near_own = pack(border_list, radiosity, air)
    near = swap(near, "district", near_pairs)
    far_small = swap(hold(far_small, own), "district", far_pairs)
    columns = end_columns(air, own)
    once = first(air, columns)
    following, ground, sides, edge, air_cell = second(air, once, patch_cell)
    far, far_own = rows(air, once)
    own = join(own, columns, near, far_small, far)
    far = hold(far, own)
    across = swap(own, "blk", [(i, i ^ 2) for i in range(blks) if i < i ^ 2])
    mine = stack(own, across, far)
    far = swap(far, "district", far_pairs)
    theirs = swap(mine, "blk", [(i, i ^ 1) for i in range(blks) if i < i ^ 1])
    radiosity, surface, air_next, side, source, ground = main(
        view_cols,
        band_weight,
        mine,
        theirs,
        reflectance,
        emissivity,
        surface_temp,
        patch_cell,
        view_factor,
        air_cell,
        ground,
        sides,
        following,
    )
    air_next, radiosity_next, surface_next = finish(
        air_next, edge, side, source, ground, radiosity, surface, near, far, near_own, far_own
    )
    return radiosity_next, surface_next, air_next


def solution(mesh):
    in_specs = (
        P(("district", "blk"), None, None, None),
        P(("district", "blk"), None),
        P(("district", "blk")),
        P(None, ("district", "blk")),
        P(None, ("district", "blk")),
        P(("district", "blk")),
        P(),
        P(("district", "blk")),
        P(("district", "blk")),
        P(None, "district", "blk"),
    )
    out_specs = (P(None, ("district", "blk")), P(("district", "blk")), P(None, "district", "blk"))
    return jax.shard_map(body, mesh=mesh, in_specs=in_specs, out_specs=out_specs, check_vma=False)
```

```python
import functools

import jax
import jax.numpy as jnp
from jax import lax
from jax.experimental import pallas as pl
from jax.experimental.pallas import tpu as pltpu
from jax.sharding import PartitionSpec as P

KAPPA = 0.15
GAIN = 0.02
COUPLE = 0.2
HEAT = 1.0
CENTRE = (1.0 - 6.0 * KAPPA) / KAPPA
SQUARE = KAPPA * KAPPA

F32 = jnp.float32
BF16 = jnp.bfloat16
LANES = 128
VMEM = pltpu.VMEM
SMEM = pltpu.SMEM
DMA = pltpu.SemaphoreType.DMA
PACK_COST, COLUMNS_COST, ROWS_COST, JOIN_COST, HOLD_COST, FIRST_COST, SECOND_COST, MAIN_COST = 2, 0.1, 1, 1, 0.1, 1, 1, 1


def params(mebibytes):
    return pltpu.CompilerParams(vmem_limit_bytes=mebibytes << 20)


def cost(microseconds):
    return pl.CostEstimate(flops=int(microseconds * 1_000_000_000), bytes_accessed=0, transcendentals=0)


def in_hbm(value):
    return pltpu.with_memory_space_constraint(value, pltpu.HBM)


WHOLE = pl.BlockSpec(memory_space=VMEM)
PLACE = pl.BlockSpec(memory_space=pl.ANY)


def iota(shape, axis):
    return lax.broadcasted_iota(jnp.int32, shape, axis)


def flag(condition):
    return jnp.where(condition, 1.0, 0.0).astype(F32)


def split(value, pieces):
    out = []
    for _ in range(pieces):
        piece = value.astype(BF16)
        out.append(piece)
        value = value - piece.astype(F32)
    return out


def plane_neighbours(load, tiles):
    centre = [load(i) for i in range(tiles)]
    rows = centre[0].shape[0]
    lane = iota((rows, LANES), 1)
    row = iota((rows, LANES), 0)
    right = [pltpu.roll(c, 1, 1) for c in centre]
    left = [pltpu.roll(c, LANES - 1, 1) for c in centre]
    zero = jnp.zeros((rows, LANES), F32)
    for i, c in enumerate(centre):
        total = jnp.where(lane == 0, right[i - 1] if i else zero, right[i])
        total = total + jnp.where(
            lane == LANES - 1, left[i + 1] if i + 1 < tiles else zero, left[i]
        )
        total = total + jnp.where(row == 0, 0.0, pltpu.roll(c, 1, 0))
        total = total + jnp.where(row == rows - 1, 0.0, pltpu.roll(c, rows - 1, 0))
        yield c, total


def start_rows(air_ref, slabs, sem, last):
    depth = air_ref.shape[1]
    for i, r in enumerate((depth - 1, depth - 2) if last else (0, 1)):
        pltpu.make_async_copy(air_ref.at[:, r, :], slabs.at[i], sem.at[i]).start()


def wait_rows(air_ref, slabs, sem):
    for i in range(2):
        pltpu.make_async_copy(air_ref.at[:, i, :], slabs.at[i], sem.at[i]).wait()


def put_rows(slabs, out_ref):
    levels, width = slabs.shape[1:]
    tiles, parts = width // LANES, levels // 16

    def lost(i):
        value = slabs[0, :, i * LANES : (i + 1) * LANES]
        return value - value.astype(BF16).astype(F32)

    for i, (c, around) in enumerate(plane_neighbours(lost, tiles)):
        at = slice(i * LANES, (i + 1) * LANES)
        values = slabs[0, :, at], slabs[1, :, at] + CENTRE * 2.0 * c + 2.0 * around
        for k, value in enumerate(values):
            value = value.astype(BF16)
            for q in range(parts):
                out_ref[(k * tiles + i) * parts + q] = value[16 * q : 16 * q + 16]


def pack_kernel(
    border_ref,
    radiosity_ref,
    air_ref,
    near_out,
    far_small,
    own_ref,
    slabs,
    border,
    blocks_of,
    ends,
    spread,
    sem,
    end_sem,
    row_sem,
):
    levels, depth, width = air_ref.shape
    blocks = radiosity_ref.shape[1] // LANES
    borders = border_ref.shape[0]
    at_small = near_out.shape[0] - far_small.shape[0]
    odd = lax.rem(lax.axis_index("district"), 2)

    @pl.when(odd == 0)
    def _():
        start_rows(air_ref, slabs, row_sem, True)

    @pl.when(odd == 1)
    def _():
        start_rows(air_ref, slabs, row_sem, False)

    first = [
        pltpu.make_async_copy(border_ref, border, sem.at[0]),
        pltpu.make_async_copy(radiosity_ref, blocks_of, sem.at[1]),
    ]
    edge = [
        pltpu.make_async_copy(
            air_ref.at[:, x, pl.ds(y, LANES)], ends.at[i, j], end_sem.at[i, j]
        )
        for i, x in enumerate((0, depth - 1))
        for j, y in enumerate((0, width - LANES))
    ]
    for c in first + edge:
        c.start()
    spread[...] = jnp.zeros(spread.shape, F32)
    for c in first:
        c.wait()
    for s in range(blocks):
        own_ref[s] = blocks_of[:, s * LANES : (s + 1) * LANES]
    for s in range(borders):
        tile = own_ref[border[s]]
        near_out[at_small + s] = tile
        far_small[s] = tile
    for c in edge:
        c.wait()
    lane = iota((levels, LANES), 1)
    sub = iota((16, LANES), 0)
    corner = []
    for i in range(2):
        spread[i, pl.ds(0, levels, 2), :] = jnp.where(lane < LANES // 2, ends[i, 0], ends[i, 1])
        turned = spread[i].T
        tile = jnp.zeros((16, LANES), F32)
        for n, row in enumerate((turned[0:1], turned[LANES - 1 : LANES])):
            high = row.astype(BF16).astype(F32)
            tile = jnp.where(sub == 2 * n, high, tile)
            tile = jnp.where(sub == 2 * n + 1, row - high, tile)
        corner.append(tile)
    near_out[at_small + borders] = jnp.where(odd == 0, corner[1], corner[0]).astype(BF16)
    far_small[borders] = jnp.where(odd == 0, corner[0], corner[1]).astype(BF16)
    wait_rows(air_ref, slabs, row_sem)
    put_rows(slabs, near_out)


def pack(border_list, radiosity, air):
    levels, _, width = air.shape
    blocks = radiosity.shape[1] // LANES
    borders = border_list.shape[0]
    row_tiles = 2 * (width // LANES) * (levels // 16)
    tile = lambda n: jax.ShapeDtypeStruct((n, 16, LANES), BF16)
    return pl.pallas_call(
        pack_kernel,
        out_shape=(
            tile(row_tiles + borders + 1),
            tile(borders + 1),
            tile(blocks),
            jax.ShapeDtypeStruct((2, levels, width), F32),
        ),
        in_specs=[PLACE] * 3,
        out_specs=(WHOLE,) * 4,
        scratch_shapes=[
            SMEM(border_list.shape, border_list.dtype),
            VMEM(radiosity.shape, BF16),
            VMEM((2, 2, levels, LANES), F32),
            VMEM((2, LANES, LANES), F32),
            DMA((2,)),
            DMA((2, 2)),
            DMA((2,)),
        ],
        compiler_params=params(8),
        cost_estimate=cost(PACK_COST),
        name="pack",
    )(in_hbm(border_list), in_hbm(radiosity), in_hbm(air))


def columns_kernel(air_ref, after_ref, columns):
    del after_ref
    levels, depth, width = air_ref.shape
    place = iota((depth, LANES), 1) // 2
    for j in range(2):
        packed = jnp.zeros((depth, LANES), F32)
        for z in range(levels):
            tile = air_ref[z, :, j * (width - LANES) : j * (width - LANES) + LANES]
            turn = (2 * z + 2 * j) % LANES
            packed = jnp.where(place == z, pltpu.roll(tile, turn, 1) if turn else tile, packed)
        for n, piece in enumerate(split(packed, 2)):
            columns[2 * j + n] = piece


def end_columns(air, after):
    return pl.pallas_call(
        columns_kernel,
        out_shape=jax.ShapeDtypeStruct((4, air.shape[1], LANES), BF16),
        in_specs=[WHOLE, PLACE],
        out_specs=WHOLE,
        compiler_params=params(8),
        cost_estimate=cost(COLUMNS_COST),
        name="columns",
    )(air, after)


def hold_kernel(value_ref, after_ref, out_ref):
    del after_ref
    out_ref[...] = value_ref[...]


def hold(value, after):
    return pl.pallas_call(
        hold_kernel,
        out_shape=jax.ShapeDtypeStruct(value.shape, value.dtype),
        in_specs=[WHOLE, PLACE],
        out_specs=WHOLE,
        compiler_params=params(8),
        cost_estimate=cost(HOLD_COST),
        name="hold",
    )(value, after)


def rows_kernel(air_ref, after_ref, out_ref, slabs, sem):
    del after_ref
    odd = lax.rem(lax.axis_index("district"), 2)

    @pl.when(odd == 1)
    def _():
        start_rows(air_ref, slabs, sem, True)

    @pl.when(odd == 0)
    def _():
        start_rows(air_ref, slabs, sem, False)

    wait_rows(air_ref, slabs, sem)
    put_rows(slabs, out_ref)


def rows(air, after):
    levels, _, width = air.shape
    count = 2 * (width // LANES) * (levels // 16)
    return pl.pallas_call(
        rows_kernel,
        out_shape=(
            jax.ShapeDtypeStruct((count, 16, LANES), BF16),
            jax.ShapeDtypeStruct((2, levels, width), F32),
        ),
        in_specs=[WHOLE, PLACE],
        out_specs=(WHOLE, WHOLE),
        scratch_shapes=[DMA((2,))],
        compiler_params=params(8),
        cost_estimate=cost(ROWS_COST),
        name="rows",
    )(air, after)


def join_kernel(own_ref, columns_ref, near_ref, far_ref, after_ref, out_ref):
    del after_ref
    odd = lax.rem(lax.axis_index("district"), 2)
    borders = far_ref.shape[0] - 1
    blocks = own_ref.shape[0]
    at_small = near_ref.shape[0] - far_ref.shape[0]
    for s in range(blocks):
        out_ref[s] = own_ref[s]
    for s in range(4):
        out_ref[blocks + 2 * borders + 2 + s] = columns_ref[s]
    for s in range(borders + 1):
        near, far = near_ref[at_small + s].astype(F32), far_ref[s].astype(F32)
        before = jnp.where(odd == 1, near, far).astype(BF16)
        after = jnp.where(odd == 1, far, near).astype(BF16)
        at = blocks + s if s < borders else blocks + 2 * borders
        out_ref[at] = before
        out_ref[at + (borders if s < borders else 1)] = after


def join(own, columns, near, far, after):
    count = own.shape[0] + columns.shape[0] + 2 * far.shape[0]
    return pl.pallas_call(
        join_kernel,
        out_shape=jax.ShapeDtypeStruct((count, 16, LANES), BF16),
        in_specs=[WHOLE] * 4 + [PLACE],
        out_specs=WHOLE,
        compiler_params=params(8),
        cost_estimate=cost(JOIN_COST),
        name="join",
    )(own, columns, near, far, after)


def stack_kernel(one_ref, two_ref, after_ref, out_ref):
    del after_ref
    part = one_ref.shape[0]
    for s in range(part):
        out_ref[s] = one_ref[s]
        out_ref[part + s] = two_ref[s]


def stack(one, two, after):
    return pl.pallas_call(
        stack_kernel,
        out_shape=jax.ShapeDtypeStruct((2 * one.shape[0], 16, LANES), BF16),
        in_specs=[WHOLE] * 2 + [PLACE],
        out_specs=WHOLE,
        compiler_params=params(8),
        cost_estimate=cost(JOIN_COST),
        name="stack",
    )(one, two, after)


def cell_masks(cell_ref, depth, width):
    patches = cell_ref.shape[0]
    cell = cell_ref[...].reshape(1, patches)
    x_of, y_of = cell // width, cell % width
    spots = iota((LANES, patches), 0)
    at_low = jnp.where(spots == y_of % LANES, 1.0, 0.0).astype(BF16)
    return at_low, spots == (y_of // LANES) * depth + x_of


def stencil_level(z, src, store):
    levels, depth, width = src.shape
    tiles = width // LANES
    half = depth // 2
    sub = iota((half, LANES), 0)
    lane = iota((half, LANES), 1)
    zero = jnp.zeros((half, LANES), F32)
    below, above = jnp.maximum(z - 1, 0), jnp.minimum(z + 1, levels - 1)
    under, over = flag(z > 0), flag(z < levels - 1)
    at = [slice(t * LANES, (t + 1) * LANES) for t in range(tiles)]
    at_x = [slice(x * half, (x + 1) * half) for x in range(2)]
    centre = [[src[z, i, j] for j in at] for i in at_x]
    for x in range(2):
        fore = [pltpu.roll(c, 1, 1) for c in centre[x]]
        back = [pltpu.roll(c, LANES - 1, 1) for c in centre[x]]
        for t in range(tiles):
            c = centre[x][t]
            before = pltpu.roll(centre[0][t], 1, 0) if x else zero
            after = zero if x else pltpu.roll(centre[1][t], half - 1, 0)
            total = src[below, at_x[x], at[t]] * under + src[above, at_x[x], at[t]] * over
            total = total + jnp.where(sub == 0, before, pltpu.roll(c, 1, 0))
            total = total + jnp.where(sub == half - 1, after, pltpu.roll(c, half - 1, 0))
            total = total + jnp.where(lane == 0, fore[t - 1] if t else zero, fore[t])
            total = total + jnp.where(
                lane == LANES - 1, back[t + 1] if t + 1 < tiles else zero, back[t]
            )
            store(x, t, total + CENTRE * c)


def first_kernel(air_ref, after_ref, once):
    del after_ref
    levels, depth, _ = air_ref.shape
    half = depth // 2

    def level(z, carry):
        def store(x, t, total):
            once[z, x * half : (x + 1) * half, t * LANES : (t + 1) * LANES] = total

        stencil_level(z, air_ref, store)
        return carry

    lax.fori_loop(0, levels, level, 0, unroll=levels // 2)


def first(air, after):
    return pl.pallas_call(
        first_kernel,
        out_shape=jax.ShapeDtypeStruct(air.shape, F32),
        in_specs=[WHOLE, PLACE],
        out_specs=WHOLE,
        compiler_params=params(12),
        cost_estimate=cost(FIRST_COST),
        name="first",
    )(air, after)


def second_kernel(
    air_ref,
    once,
    cell_ref,
    air_out,
    ground_out,
    sides_out,
    edge_out,
    cell_out,
    result,
    out_sem,
    edge_sem,
    *,
    spans,
):
    levels, depth, width = once.shape
    tiles = width // LANES
    half = depth // 2
    at = [slice(t * LANES, (t + 1) * LANES) for t in range(tiles)]
    at_x = [slice(x * half, (x + 1) * half) for x in range(2)]

    def level(z, carry):
        def store(x, t, total):
            total = SQUARE * total
            result[z, at_x[x], at[t]] = total
            if t in (0, tiles - 1):
                sides_out[0 if t == 0 else 1, z, at_x[x]] = total

        stencil_level(z, once, store)
        return carry

    writes = []
    done = 0
    for k, count in enumerate(spans):
        lax.fori_loop(done, done + count, level, 0, unroll=count)
        span = pl.ds(done, count)
        done += count
        lanes = pl.ds(LANES, width - 2 * LANES)
        c = pltpu.make_async_copy(
            result.at[span, :, lanes], air_out.at[span, :, lanes], out_sem.at[k]
        )
        c.start()
        writes.append(c)
    for i, x in enumerate((0, 1, depth - 2, depth - 1)):
        c = pltpu.make_async_copy(result.at[:, x, lanes], edge_out.at[i], edge_sem.at[i])
        c.start()
        writes.append(c)
    ground_out[...] = result[0]
    at_low, at_high = cell_masks(cell_ref, depth, width)
    ground = jnp.concatenate([air_ref[0, :, j] for j in at], axis=0)
    picked = sum(
        jnp.dot(piece, at_low, preferred_element_type=F32) for piece in split(ground, 3)
    )
    cell_out[...] = jnp.sum(jnp.where(at_high, picked, 0.0), axis=0, keepdims=True)
    for c in writes:
        c.wait()


def second(air, once, cell):
    levels, depth, width = air.shape
    spans = (levels // 2, levels // 4, levels // 8, levels // 8)
    return pl.pallas_call(
        functools.partial(second_kernel, spans=spans),
        out_shape=(
            jax.ShapeDtypeStruct(air.shape, F32),
            jax.ShapeDtypeStruct((depth, width), F32),
            jax.ShapeDtypeStruct((2, levels, depth, LANES), F32),
            jax.ShapeDtypeStruct((4, levels, width - 2 * LANES), F32),
            jax.ShapeDtypeStruct((1, cell.shape[0]), F32),
        ),
        in_specs=[WHOLE] * 3,
        out_specs=(PLACE,) + (WHOLE,) * 4,
        scratch_shapes=[VMEM(air.shape, F32), DMA((len(spans),)), DMA((4,))],
        compiler_params=params(20),
        cost_estimate=cost(SECOND_COST),
        name="second",
    )(air, once, cell)


def main_kernel(
    cols_ref,
    weight_ref,
    mine_ref,
    theirs_ref,
    reflectance_ref,
    emissivity_ref,
    temp_ref,
    cell_ref,
    view_ref,
    air_cell_ref,
    ground_ref,
    sides_ref,
    next_ref,
    radiosity_out,
    surface_out,
    air_out,
    side_edge_out,
    source_out,
    ground_out,
    sides,
    pieces,
    out_sem,
):
    del next_ref
    levels, depth = sides_ref.shape[1:3]
    width = ground_ref.shape[1]
    tiles = width // LANES
    row_blocks, nonzero = view_ref.shape[0], view_ref.shape[1]
    blk = lax.axis_index("blk")
    blks = lax.axis_size("blk")
    has_left, has_right = flag(blk > 0), flag(blk < blks - 1)
    part = mine_ref.shape[0] // 2
    visible = part - 6
    for n, (ref, base) in enumerate(
        ((mine_ref, 0), (theirs_ref, 0), (mine_ref, part), (theirs_ref, part))
    ):
        for s in range(visible):
            pieces[n * visible + s] = ref[base + s]

    writes = []
    even = lax.rem(blk, 2) == 0

    def pair(ref, at):
        return ref[at].astype(F32) + ref[at + 1].astype(F32)

    def received(load):
        one, three = load(0), load(part)
        return jnp.where(even, three, one) * has_left, jnp.where(even, one, three) * has_right

    columns = [received(lambda base, n=n: pair(theirs_ref, base + visible + 2 + n)) for n in (0, 2)]
    corners = [received(lambda base, n=n: theirs_ref[base + visible + n].astype(F32)) for n in (0, 1)]
    sub = iota((depth, LANES), 0)
    lane = iota((depth, LANES), 1)
    half = depth // 2
    beside = []
    for side in range(2):
        k = 2 if side == 0 else 0
        shift = LANES - 1 if side == 0 else 0
        turn = lambda v: pltpu.roll(v, shift, 1) if shift else v
        near = turn(columns[1 - side][side])
        beyond = columns[1][0] if side == 0 else pltpu.roll(columns[0][1], LANES - 1, 1)
        own = pair(mine_ref, visible + 2 + 2 * side)
        own = own if side == 0 else pltpu.roll(own, LANES - 1, 1)
        top, bottom = (c[side][k : k + 1] + c[side][k + 1 : k + 2] for c in corners)
        around = jnp.where(sub == 0, top, pltpu.roll(near, 1, 0))
        around = around + jnp.where(sub == depth - 1, bottom, pltpu.roll(near, depth - 1, 0))
        around = around + jnp.where(lane < 2, 0.0, pltpu.roll(near, 2, 1))
        around = around + jnp.where(lane >= 2 * levels - 2, 0.0, pltpu.roll(near, LANES - 2, 1))
        outer = 2.0 * CENTRE * near + 2.0 * around + beyond + own * (has_right if side else has_left)
        if side == 0:
            value = jnp.where(lane % 2 == 0, outer, pltpu.roll(near, 1, 1))
        else:
            value = jnp.where(lane % 2 == 0, near, pltpu.roll(outer, 1, 1))
        beside.append(SQUARE * value)

    lane8 = iota((half, LANES), 1)
    both = [lane8 < 2, lane8 >= LANES - 2]

    for z in range(levels):
        for side in range(2):
            turn = (2 * LANES - 2 * z - 2 * side) % LANES
            for x in range(2):
                at = slice(x * half, (x + 1) * half)
                value = pltpu.roll(beside[side][at], turn, 1) if turn else beside[side][at]
                value = sides_ref[side, z, at] + jnp.where(both[side], value, 0.0)
                sides[side, z, at] = value
                for i, row in ((2, half - 2), (3, half - 1)) if x else ((0, 0), (1, 1)):
                    side_edge_out[side, i, z : z + 1] = value[row : row + 1]
    for side in range(2):
        lanes = pl.ds(side * (width - LANES), LANES)
        c = pltpu.make_async_copy(
            sides.at[side, pl.ds(1, levels - 1)],
            air_out.at[pl.ds(1, levels - 1), :, lanes],
            out_sem.at[side],
        )
        c.start()
        writes.append(c)
    blocks = []
    for r in range(row_blocks):
        picked = []
        for k in range(nonzero):
            c = cols_ref[r, k]
            owner = c // visible
            picked.append(pieces[jnp.bitwise_xor(owner, blk) * visible + (c - owner * visible)])
        blocks.append(
            lax.dot_general(
                jnp.concatenate(picked, axis=1),
                jnp.concatenate([view_ref[r, k] for k in range(nonzero)], axis=1),
                (((1,), (1,)), ((), ())),
                preferred_element_type=F32,
            )
        )
    irradiance = jnp.concatenate(blocks, axis=1)

    patches = cell_ref.shape[0]
    at_low, at_high = cell_masks(cell_ref, depth, width)
    air_cell = air_cell_ref[...]
    temp = temp_ref[...].reshape(1, patches)
    squared = temp * temp
    bands = reflectance_ref.shape[0]
    weight = jnp.zeros((bands, LANES), F32)
    for n in range(bands):
        weight = jnp.where(iota((bands, LANES), 0) == n, weight_ref[n], weight)
    weight = jnp.concatenate([weight] * (patches // LANES), axis=1)
    emission = weight * (emissivity_ref[...].reshape(1, patches) * (squared * squared))
    albedo = reflectance_ref[...].astype(F32)
    radiosity_out[...] = emission + albedo * irradiance
    absorbed = jnp.sum((1.0 - albedo) * irradiance, axis=0, keepdims=True)
    emitted = jnp.sum(emission, axis=0, keepdims=True)
    surface = temp + GAIN * (absorbed - emitted) - COUPLE * (temp - 1.0 - air_cell)
    surface_out[...] = surface
    flux = HEAT * (COUPLE * (surface - 1.0 - air_cell))
    source = sum(
        lax.dot_general(
            jnp.where(at_high, piece.astype(F32), 0.0).astype(BF16),
            at_low,
            (((1,), (1,)), ((), ())),
            preferred_element_type=F32,
        )
        for piece in split(flux, 2)
    )

    for t in range(tiles):
        at = slice(t * LANES, (t + 1) * LANES)
        here = source[t * depth : (t + 1) * depth]
        before = sides[0 if t == 0 else 1, 0] if t in (0, tiles - 1) else ground_ref[:, at]
        ground_out[:, at] = before + here
        for i, x in enumerate((0, 1, depth - 2, depth - 1)):
            source_out[i : i + 1, at] = here[x : x + 1]
    for c in writes:
        c.wait()


def main(
    cols, weight, mine, theirs, reflectance, emissivity, temp, cell, view, air_cell, ground, sides, following
):
    levels, depth = sides.shape[1:3]
    width = ground.shape[1]
    bands, patches = reflectance.shape
    visible = mine.shape[0] // 2 - 6
    return pl.pallas_call(
        main_kernel,
        out_shape=(
            jax.ShapeDtypeStruct((bands, patches), F32),
            jax.ShapeDtypeStruct((1, patches), F32),
            jax.ShapeDtypeStruct(following.shape, F32),
            jax.ShapeDtypeStruct((2, 4, levels, LANES), F32),
            jax.ShapeDtypeStruct((4, width), F32),
            jax.ShapeDtypeStruct((depth, width), F32),
        ),
        in_specs=[pl.BlockSpec(memory_space=SMEM)] * 2 + [WHOLE] * 10 + [PLACE],
        out_specs=(WHOLE, WHOLE, PLACE, WHOLE, WHOLE, WHOLE),
        scratch_shapes=[
            VMEM(sides.shape, F32),
            VMEM((4 * visible, 16, LANES), BF16),
            DMA((2,)),
        ],
        input_output_aliases={12: 2},
        compiler_params=params(20),
        cost_estimate=cost(MAIN_COST),
        name="main",
    )(
        cols,
        weight,
        mine,
        theirs,
        reflectance,
        emissivity,
        temp,
        cell,
        view,
        air_cell,
        ground,
        sides,
        in_hbm(following),
    )


def finish_kernel(
    air_ref,
    edge_ref,
    side_ref,
    source_ref,
    ground_ref,
    radiosity_ref,
    surface_ref,
    near_ref,
    far_ref,
    near_own,
    far_own,
    out_ref,
    radiosity_out,
    surface_out,
    slabs,
    sem,
    value_sem,
):
    del air_ref
    levels, depth, width = out_ref.shape
    parts = levels // 16
    tiles = width // LANES
    district = lax.axis_index("district")
    odd = lax.rem(district, 2)
    has = flag(district > 0), flag(district < lax.axis_size("district") - 1)
    ground = iota((levels, LANES), 0) == 0
    copies = [
        pltpu.make_async_copy(ground_ref.at[x], out_ref.at[0, x], sem.at[2 + x])
        for x in range(2, depth - 2)
    ]
    copies += [
        pltpu.make_async_copy(radiosity_ref, radiosity_out, value_sem.at[0]),
        pltpu.make_async_copy(surface_ref.at[0], surface_out, value_sem.at[1]),
    ]
    for c in copies:
        c.start()
    for side in range(2):
        use_near = (odd == 1) if side == 0 else (odd == 0)

        def received(k, i):
            at = [(k * tiles + i) * parts + q for q in range(parts)]
            near, far = (jnp.concatenate([ref[n] for n in at]) for ref in (near_ref, far_ref))
            return jnp.where(use_near, near.astype(F32), far.astype(F32))

        def base(n, i):
            if i in (0, tiles - 1):
                value = side_ref[0 if i == 0 else 1, n]
            else:
                value = edge_ref[n, :, (i - 1) * LANES : i * LANES]
            return value + jnp.where(ground, source_ref[n : n + 1, i * LANES : (i + 1) * LANES], 0.0)

        outer, inner = (0, 1) if side == 0 else (3, 2)
        for i, (c, around) in enumerate(plane_neighbours(functools.partial(received, 0), tiles)):
            at = slice(i * LANES, (i + 1) * LANES)
            own = jnp.where(use_near, near_own[0, :, at], far_own[0, :, at]) * has[side]
            reach = (2.0 * CENTRE) * c + 2.0 * around + received(1, i) + own
            slabs[outer, :, at] = base(outer, i) + SQUARE * reach
            slabs[inner, :, at] = base(inner, i) + SQUARE * c
        for i in (outer, inner):
            x = (0, 1, depth - 2, depth - 1)[i]
            c = pltpu.make_async_copy(slabs.at[i], out_ref.at[:, x, :], sem.at[i])
            c.start()
            copies.append(c)
    for c in copies:
        c.wait()


def finish(air, edge, side, source, ground, radiosity, surface, near, far, near_own, far_own):
    levels, depth, width = air.shape
    return pl.pallas_call(
        finish_kernel,
        out_shape=(
            jax.ShapeDtypeStruct(air.shape, F32),
            jax.ShapeDtypeStruct(radiosity.shape, F32),
            jax.ShapeDtypeStruct(surface.shape[1:], F32),
        ),
        in_specs=[PLACE] + [WHOLE] * 10,
        out_specs=(PLACE,) * 3,
        scratch_shapes=[VMEM((4, levels, width), F32), DMA((depth,)), DMA((2,))],
        input_output_aliases={0: 0},
        compiler_params=params(8),
        name="finish",
    )(in_hbm(air), edge, side, source, ground, radiosity, surface, near, far, near_own, far_own)


def swap(value, axis, pairs):
    return lax.ppermute(value, axis, [p for a, b in pairs for p in ((a, b), (b, a))])


def body(
    view_factor,
    view_cols,
    border_list,
    radiosity,
    reflectance,
    emissivity,
    band_weight,
    surface_temp,
    patch_cell,
    air,
):
    districts, blks = lax.axis_size("district"), lax.axis_size("blk")
    near_pairs = [(i, i + 1) for i in range(0, districts - 1, 2)]
    far_pairs = [(i, i + 1) for i in range(1, districts - 1, 2)]
    near, far_small, own, near_own = pack(border_list, radiosity, air)
    near = swap(near, "district", near_pairs)
    far_small = swap(hold(far_small, own), "district", far_pairs)
    columns = end_columns(air, own)
    once = first(air, columns)
    following, ground, sides, edge, air_cell = second(air, once, patch_cell)
    far, far_own = rows(air, once)
    own = join(own, columns, near, far_small, far)
    far = hold(far, own)
    across = swap(own, "blk", [(i, i ^ 2) for i in range(blks) if i < i ^ 2])
    mine = stack(own, across, far)
    far = swap(far, "district", far_pairs)
    theirs = swap(mine, "blk", [(i, i ^ 1) for i in range(blks) if i < i ^ 1])
    radiosity, surface, air_next, side, source, ground = main(
        view_cols,
        band_weight,
        mine,
        theirs,
        reflectance,
        emissivity,
        surface_temp,
        patch_cell,
        view_factor,
        air_cell,
        ground,
        sides,
        following,
    )
    air_next, radiosity_next, surface_next = finish(
        air_next, edge, side, source, ground, radiosity, surface, near, far, near_own, far_own
    )
    return radiosity_next, surface_next, air_next


def solution(mesh):
    in_specs = (
        P(("district", "blk"), None, None, None),
        P(("district", "blk"), None),
        P(("district", "blk")),
        P(None, ("district", "blk")),
        P(None, ("district", "blk")),
        P(("district", "blk")),
        P(),
        P(("district", "blk")),
        P(("district", "blk")),
        P(None, "district", "blk"),
    )
    out_specs = (P(None, ("district", "blk")), P(("district", "blk")), P(None, "district", "blk"))
    return jax.shard_map(body, mesh=mesh, in_specs=in_specs, out_specs=out_specs, check_vma=False)
```

```python
import functools

import jax
import jax.numpy as jnp
from jax import lax
from jax.experimental import pallas as pl
from jax.experimental.pallas import tpu as pltpu
from jax.sharding import PartitionSpec as P

KAPPA = 0.15
GAIN = 0.02
COUPLE = 0.2
HEAT = 1.0
CENTRE = (1.0 - 6.0 * KAPPA) / KAPPA
SQUARE = KAPPA * KAPPA

F32 = jnp.float32
BF16 = jnp.bfloat16
LANES = 128
VMEM = pltpu.VMEM
SMEM = pltpu.SMEM
DMA = pltpu.SemaphoreType.DMA
PACK_COST, COLUMNS_COST, ROWS_COST, JOIN_COST, HOLD_COST, FIRST_COST, SECOND_COST, MAIN_COST = 2, 0.1, 1, 1, 0.1, 1, 1, 1


def params(mebibytes):
    return pltpu.CompilerParams(vmem_limit_bytes=mebibytes << 20)


def cost(microseconds):
    return pl.CostEstimate(flops=int(microseconds * 1_000_000_000), bytes_accessed=0, transcendentals=0)


def in_hbm(value):
    return pltpu.with_memory_space_constraint(value, pltpu.HBM)


WHOLE = pl.BlockSpec(memory_space=VMEM)
PLACE = pl.BlockSpec(memory_space=pl.ANY)


def iota(shape, axis):
    return lax.broadcasted_iota(jnp.int32, shape, axis)


def flag(condition):
    return jnp.where(condition, 1.0, 0.0).astype(F32)


def split(value, pieces):
    out = []
    for _ in range(pieces):
        piece = value.astype(BF16)
        out.append(piece)
        value = value - piece.astype(F32)
    return out


def plane_neighbours(load, tiles):
    centre = [load(i) for i in range(tiles)]
    rows = centre[0].shape[0]
    lane = iota((rows, LANES), 1)
    row = iota((rows, LANES), 0)
    right = [pltpu.roll(c, 1, 1) for c in centre]
    left = [pltpu.roll(c, LANES - 1, 1) for c in centre]
    zero = jnp.zeros((rows, LANES), F32)
    for i, c in enumerate(centre):
        total = jnp.where(lane == 0, right[i - 1] if i else zero, right[i])
        total = total + jnp.where(
            lane == LANES - 1, left[i + 1] if i + 1 < tiles else zero, left[i]
        )
        total = total + jnp.where(row == 0, 0.0, pltpu.roll(c, 1, 0))
        total = total + jnp.where(row == rows - 1, 0.0, pltpu.roll(c, rows - 1, 0))
        yield c, total


def start_rows(air_ref, slabs, sem, last):
    depth = air_ref.shape[1]
    for i, r in enumerate((depth - 1, depth - 2) if last else (0, 1)):
        pltpu.make_async_copy(air_ref.at[:, r, :], slabs.at[i], sem.at[i]).start()


def wait_rows(air_ref, slabs, sem):
    for i in range(2):
        pltpu.make_async_copy(air_ref.at[:, i, :], slabs.at[i], sem.at[i]).wait()


def put_rows(slabs, out_ref):
    levels, width = slabs.shape[1:]
    tiles, parts = width // LANES, levels // 16

    def lost(i):
        value = slabs[0, :, i * LANES : (i + 1) * LANES]
        return value - value.astype(BF16).astype(F32)

    for i, (c, around) in enumerate(plane_neighbours(lost, tiles)):
        at = slice(i * LANES, (i + 1) * LANES)
        values = slabs[0, :, at], slabs[1, :, at] + CENTRE * 2.0 * c + 2.0 * around
        for k, value in enumerate(values):
            value = value.astype(BF16)
            for q in range(parts):
                out_ref[(k * tiles + i) * parts + q] = value[16 * q : 16 * q + 16]


def pack_kernel(
    border_ref,
    radiosity_ref,
    air_ref,
    near_out,
    far_small,
    own_ref,
    slabs,
    border,
    blocks_of,
    ends,
    spread,
    sem,
    end_sem,
    row_sem,
):
    levels, depth, width = air_ref.shape
    blocks = radiosity_ref.shape[1] // LANES
    borders = border_ref.shape[0]
    at_small = near_out.shape[0] - far_small.shape[0]
    odd = lax.rem(lax.axis_index("district"), 2)

    @pl.when(odd == 0)
    def _():
        start_rows(air_ref, slabs, row_sem, True)

    @pl.when(odd == 1)
    def _():
        start_rows(air_ref, slabs, row_sem, False)

    first = [
        pltpu.make_async_copy(border_ref, border, sem.at[0]),
        pltpu.make_async_copy(radiosity_ref, blocks_of, sem.at[1]),
    ]
    edge = [
        pltpu.make_async_copy(
            air_ref.at[:, x, pl.ds(y, LANES)], ends.at[i, j], end_sem.at[i, j]
        )
        for i, x in enumerate((0, depth - 1))
        for j, y in enumerate((0, width - LANES))
    ]
    for c in first + edge:
        c.start()
    spread[...] = jnp.zeros(spread.shape, F32)
    for c in first:
        c.wait()
    for s in range(blocks):
        own_ref[s] = blocks_of[:, s * LANES : (s + 1) * LANES]
    for s in range(borders):
        tile = own_ref[border[s]]
        near_out[at_small + s] = tile
        far_small[s] = tile
    for c in edge:
        c.wait()
    lane = iota((levels, LANES), 1)
    sub = iota((16, LANES), 0)
    corner = []
    for i in range(2):
        spread[i, pl.ds(0, levels, 2), :] = jnp.where(lane < LANES // 2, ends[i, 0], ends[i, 1])
        turned = spread[i].T
        tile = jnp.zeros((16, LANES), F32)
        for n, row in enumerate((turned[0:1], turned[LANES - 1 : LANES])):
            high = row.astype(BF16).astype(F32)
            tile = jnp.where(sub == 2 * n, high, tile)
            tile = jnp.where(sub == 2 * n + 1, row - high, tile)
        corner.append(tile)
    near_out[at_small + borders] = jnp.where(odd == 0, corner[1], corner[0]).astype(BF16)
    far_small[borders] = jnp.where(odd == 0, corner[0], corner[1]).astype(BF16)
    wait_rows(air_ref, slabs, row_sem)
    put_rows(slabs, near_out)


def pack(border_list, radiosity, air):
    levels, _, width = air.shape
    blocks = radiosity.shape[1] // LANES
    borders = border_list.shape[0]
    row_tiles = 2 * (width // LANES) * (levels // 16)
    tile = lambda n: jax.ShapeDtypeStruct((n, 16, LANES), BF16)
    return pl.pallas_call(
        pack_kernel,
        out_shape=(
            tile(row_tiles + borders + 1),
            tile(borders + 1),
            tile(blocks),
            jax.ShapeDtypeStruct((2, levels, width), F32),
        ),
        in_specs=[PLACE] * 3,
        out_specs=(WHOLE,) * 4,
        scratch_shapes=[
            SMEM(border_list.shape, border_list.dtype),
            VMEM(radiosity.shape, BF16),
            VMEM((2, 2, levels, LANES), F32),
            VMEM((2, LANES, LANES), F32),
            DMA((2,)),
            DMA((2, 2)),
            DMA((2,)),
        ],
        compiler_params=params(8),
        cost_estimate=cost(PACK_COST),
        name="pack",
    )(in_hbm(border_list), in_hbm(radiosity), in_hbm(air))


def columns_kernel(air_ref, after_ref, columns):
    del after_ref
    levels, depth, width = air_ref.shape
    place = iota((depth, LANES), 1) // 2
    for j in range(2):
        packed = jnp.zeros((depth, LANES), F32)
        for z in range(levels):
            tile = air_ref[z, :, j * (width - LANES) : j * (width - LANES) + LANES]
            turn = (2 * z + 2 * j) % LANES
            packed = jnp.where(place == z, pltpu.roll(tile, turn, 1) if turn else tile, packed)
        for n, piece in enumerate(split(packed, 2)):
            columns[2 * j + n] = piece


def end_columns(air, after):
    return pl.pallas_call(
        columns_kernel,
        out_shape=jax.ShapeDtypeStruct((4, air.shape[1], LANES), BF16),
        in_specs=[WHOLE, PLACE],
        out_specs=WHOLE,
        compiler_params=params(8),
        cost_estimate=cost(COLUMNS_COST),
        name="columns",
    )(air, after)


def hold_kernel(value_ref, after_ref, out_ref):
    del after_ref
    out_ref[...] = value_ref[...]


def hold(value, after):
    return pl.pallas_call(
        hold_kernel,
        out_shape=jax.ShapeDtypeStruct(value.shape, value.dtype),
        in_specs=[WHOLE, PLACE],
        out_specs=WHOLE,
        compiler_params=params(8),
        cost_estimate=cost(HOLD_COST),
        name="hold",
    )(value, after)


def rows_kernel(air_ref, after_ref, out_ref, slabs, sem):
    del after_ref
    odd = lax.rem(lax.axis_index("district"), 2)

    @pl.when(odd == 1)
    def _():
        start_rows(air_ref, slabs, sem, True)

    @pl.when(odd == 0)
    def _():
        start_rows(air_ref, slabs, sem, False)

    wait_rows(air_ref, slabs, sem)
    put_rows(slabs, out_ref)


def rows(air, after):
    levels, _, width = air.shape
    count = 2 * (width // LANES) * (levels // 16)
    return pl.pallas_call(
        rows_kernel,
        out_shape=(
            jax.ShapeDtypeStruct((count, 16, LANES), BF16),
            jax.ShapeDtypeStruct((2, levels, width), F32),
        ),
        in_specs=[WHOLE, PLACE],
        out_specs=(WHOLE, WHOLE),
        scratch_shapes=[DMA((2,))],
        compiler_params=params(8),
        cost_estimate=cost(ROWS_COST),
        name="rows",
    )(air, after)


def join_kernel(own_ref, columns_ref, near_ref, far_ref, after_ref, out_ref):
    del after_ref
    odd = lax.rem(lax.axis_index("district"), 2)
    borders = far_ref.shape[0] - 1
    blocks = own_ref.shape[0]
    at_small = near_ref.shape[0] - far_ref.shape[0]
    for s in range(blocks):
        out_ref[s] = own_ref[s]
    for s in range(4):
        out_ref[blocks + 2 * borders + 2 + s] = columns_ref[s]
    for s in range(borders + 1):
        near, far = near_ref[at_small + s].astype(F32), far_ref[s].astype(F32)
        before = jnp.where(odd == 1, near, far).astype(BF16)
        after = jnp.where(odd == 1, far, near).astype(BF16)
        at = blocks + s if s < borders else blocks + 2 * borders
        out_ref[at] = before
        out_ref[at + (borders if s < borders else 1)] = after


def join(own, columns, near, far, after):
    count = own.shape[0] + columns.shape[0] + 2 * far.shape[0]
    return pl.pallas_call(
        join_kernel,
        out_shape=jax.ShapeDtypeStruct((count, 16, LANES), BF16),
        in_specs=[WHOLE] * 4 + [PLACE],
        out_specs=WHOLE,
        compiler_params=params(8),
        cost_estimate=cost(JOIN_COST),
        name="join",
    )(own, columns, near, far, after)


def stack_kernel(one_ref, two_ref, after_ref, out_ref):
    del after_ref
    part = one_ref.shape[0]
    for s in range(part):
        out_ref[s] = one_ref[s]
        out_ref[part + s] = two_ref[s]


def stack(one, two, after):
    return pl.pallas_call(
        stack_kernel,
        out_shape=jax.ShapeDtypeStruct((2 * one.shape[0], 16, LANES), BF16),
        in_specs=[WHOLE] * 2 + [PLACE],
        out_specs=WHOLE,
        compiler_params=params(8),
        cost_estimate=cost(JOIN_COST),
        name="stack",
    )(one, two, after)


def cell_masks(cell_ref, depth, width):
    patches = cell_ref.shape[0]
    cell = cell_ref[...].reshape(1, patches)
    x_of, y_of = cell // width, cell % width
    spots = iota((LANES, patches), 0)
    at_low = jnp.where(spots == y_of % LANES, 1.0, 0.0).astype(BF16)
    return at_low, spots == (y_of // LANES) * depth + x_of


def stencil_level(z, src, store):
    levels, depth, width = src.shape
    tiles = width // LANES
    half = depth // 2
    sub = iota((half, LANES), 0)
    lane = iota((half, LANES), 1)
    zero = jnp.zeros((half, LANES), F32)
    below, above = jnp.maximum(z - 1, 0), jnp.minimum(z + 1, levels - 1)
    under, over = flag(z > 0), flag(z < levels - 1)
    at = [slice(t * LANES, (t + 1) * LANES) for t in range(tiles)]
    at_x = [slice(x * half, (x + 1) * half) for x in range(2)]
    centre = [[src[z, i, j] for j in at] for i in at_x]
    for x in range(2):
        fore = [pltpu.roll(c, 1, 1) for c in centre[x]]
        back = [pltpu.roll(c, LANES - 1, 1) for c in centre[x]]
        for t in range(tiles):
            c = centre[x][t]
            before = pltpu.roll(centre[0][t], 1, 0) if x else zero
            after = zero if x else pltpu.roll(centre[1][t], half - 1, 0)
            total = src[below, at_x[x], at[t]] * under + src[above, at_x[x], at[t]] * over
            total = total + jnp.where(sub == 0, before, pltpu.roll(c, 1, 0))
            total = total + jnp.where(sub == half - 1, after, pltpu.roll(c, half - 1, 0))
            total = total + jnp.where(lane == 0, fore[t - 1] if t else zero, fore[t])
            total = total + jnp.where(
                lane == LANES - 1, back[t + 1] if t + 1 < tiles else zero, back[t]
            )
            store(x, t, total + CENTRE * c)


def first_kernel(air_ref, after_ref, once):
    del after_ref
    levels, depth, _ = air_ref.shape
    half = depth // 2

    def level(z, carry):
        def store(x, t, total):
            once[z, x * half : (x + 1) * half, t * LANES : (t + 1) * LANES] = total

        stencil_level(z, air_ref, store)
        return carry

    lax.fori_loop(0, levels, level, 0, unroll=levels // 2)


def first(air, after):
    return pl.pallas_call(
        first_kernel,
        out_shape=jax.ShapeDtypeStruct(air.shape, F32),
        in_specs=[WHOLE, PLACE],
        out_specs=WHOLE,
        compiler_params=params(12),
        cost_estimate=cost(FIRST_COST),
        name="first",
    )(air, after)


def second_kernel(
    air_ref,
    once,
    cell_ref,
    air_out,
    ground_out,
    sides_out,
    edge_out,
    cell_out,
    result,
    out_sem,
    edge_sem,
    *,
    spans,
):
    levels, depth, width = once.shape
    tiles = width // LANES
    half = depth // 2
    at = [slice(t * LANES, (t + 1) * LANES) for t in range(tiles)]
    at_x = [slice(x * half, (x + 1) * half) for x in range(2)]

    def level(z, carry):
        def store(x, t, total):
            total = SQUARE * total
            result[z, at_x[x], at[t]] = total
            if t in (0, tiles - 1):
                sides_out[0 if t == 0 else 1, z, at_x[x]] = total

        stencil_level(z, once, store)
        return carry

    writes = []
    done = 0
    for k, count in enumerate(spans):
        lax.fori_loop(done, done + count, level, 0, unroll=count)
        span = pl.ds(done, count)
        done += count
        lanes = pl.ds(LANES, width - 2 * LANES)
        c = pltpu.make_async_copy(
            result.at[span, :, lanes], air_out.at[span, :, lanes], out_sem.at[k]
        )
        c.start()
        writes.append(c)
    for i, x in enumerate((0, 1, depth - 2, depth - 1)):
        c = pltpu.make_async_copy(result.at[:, x, lanes], edge_out.at[i], edge_sem.at[i])
        c.start()
        writes.append(c)
    ground_out[...] = result[0]
    at_low, at_high = cell_masks(cell_ref, depth, width)
    ground = jnp.concatenate([air_ref[0, :, j] for j in at], axis=0)
    picked = sum(
        jnp.dot(piece, at_low, preferred_element_type=F32) for piece in split(ground, 3)
    )
    cell_out[...] = jnp.sum(jnp.where(at_high, picked, 0.0), axis=0, keepdims=True)
    for c in writes:
        c.wait()


def second(air, once, cell):
    levels, depth, width = air.shape
    spans = (levels // 2, levels // 4, levels // 8, levels // 8)
    return pl.pallas_call(
        functools.partial(second_kernel, spans=spans),
        out_shape=(
            jax.ShapeDtypeStruct(air.shape, F32),
            jax.ShapeDtypeStruct((depth, width), F32),
            jax.ShapeDtypeStruct((2, levels, depth, LANES), F32),
            jax.ShapeDtypeStruct((4, levels, width - 2 * LANES), F32),
            jax.ShapeDtypeStruct((1, cell.shape[0]), F32),
        ),
        in_specs=[WHOLE] * 3,
        out_specs=(PLACE,) + (WHOLE,) * 4,
        scratch_shapes=[VMEM(air.shape, F32), DMA((len(spans),)), DMA((4,))],
        compiler_params=params(20),
        cost_estimate=cost(SECOND_COST),
        name="second",
    )(air, once, cell)


def main_kernel(
    cols_ref,
    weight_ref,
    mine_ref,
    theirs_ref,
    reflectance_ref,
    emissivity_ref,
    temp_ref,
    cell_ref,
    view_ref,
    air_cell_ref,
    ground_ref,
    sides_ref,
    next_ref,
    radiosity_out,
    surface_out,
    air_out,
    side_edge_out,
    source_out,
    ground_out,
    sides,
    pieces,
    out_sem,
):
    del next_ref
    levels, depth = sides_ref.shape[1:3]
    width = ground_ref.shape[1]
    tiles = width // LANES
    row_blocks, nonzero = view_ref.shape[0], view_ref.shape[1]
    blk = lax.axis_index("blk")
    blks = lax.axis_size("blk")
    has_left, has_right = flag(blk > 0), flag(blk < blks - 1)
    part = mine_ref.shape[0] // 2
    visible = part - 6
    for n, (ref, base) in enumerate(
        ((mine_ref, 0), (theirs_ref, 0), (mine_ref, part), (theirs_ref, part))
    ):
        for s in range(visible):
            pieces[n * visible + s] = ref[base + s]

    writes = []
    even = lax.rem(blk, 2) == 0

    def pair(ref, at):
        return ref[at].astype(F32) + ref[at + 1].astype(F32)

    def received(load):
        one, three = load(0), load(part)
        return jnp.where(even, three, one) * has_left, jnp.where(even, one, three) * has_right

    columns = [received(lambda base, n=n: pair(theirs_ref, base + visible + 2 + n)) for n in (0, 2)]
    corners = [received(lambda base, n=n: theirs_ref[base + visible + n].astype(F32)) for n in (0, 1)]
    sub = iota((depth, LANES), 0)
    lane = iota((depth, LANES), 1)
    half = depth // 2
    beside = []
    for side in range(2):
        k = 2 if side == 0 else 0
        shift = LANES - 1 if side == 0 else 0
        turn = lambda v: pltpu.roll(v, shift, 1) if shift else v
        near = turn(columns[1 - side][side])
        beyond = columns[1][0] if side == 0 else pltpu.roll(columns[0][1], LANES - 1, 1)
        own = pair(mine_ref, visible + 2 + 2 * side)
        own = own if side == 0 else pltpu.roll(own, LANES - 1, 1)
        top, bottom = (c[side][k : k + 1] + c[side][k + 1 : k + 2] for c in corners)
        around = jnp.where(sub == 0, top, pltpu.roll(near, 1, 0))
        around = around + jnp.where(sub == depth - 1, bottom, pltpu.roll(near, depth - 1, 0))
        around = around + jnp.where(lane < 2, 0.0, pltpu.roll(near, 2, 1))
        around = around + jnp.where(lane >= 2 * levels - 2, 0.0, pltpu.roll(near, LANES - 2, 1))
        outer = 2.0 * CENTRE * near + 2.0 * around + beyond + own * (has_right if side else has_left)
        if side == 0:
            value = jnp.where(lane % 2 == 0, outer, pltpu.roll(near, 1, 1))
        else:
            value = jnp.where(lane % 2 == 0, near, pltpu.roll(outer, 1, 1))
        beside.append(SQUARE * value)

    lane8 = iota((half, LANES), 1)
    both = [lane8 < 2, lane8 >= LANES - 2]

    for z in range(levels):
        for side in range(2):
            turn = (2 * LANES - 2 * z - 2 * side) % LANES
            for x in range(2):
                at = slice(x * half, (x + 1) * half)
                value = pltpu.roll(beside[side][at], turn, 1) if turn else beside[side][at]
                value = sides_ref[side, z, at] + jnp.where(both[side], value, 0.0)
                sides[side, z, at] = value
                for i, row in ((2, half - 2), (3, half - 1)) if x else ((0, 0), (1, 1)):
                    side_edge_out[side, i, z : z + 1] = value[row : row + 1]
    for side in range(2):
        lanes = pl.ds(side * (width - LANES), LANES)
        c = pltpu.make_async_copy(
            sides.at[side, pl.ds(1, levels - 1)],
            air_out.at[pl.ds(1, levels - 1), :, lanes],
            out_sem.at[side],
        )
        c.start()
        writes.append(c)
    blocks = []
    for r in range(row_blocks):
        picked = []
        for k in range(nonzero):
            c = cols_ref[r, k]
            owner = c // visible
            picked.append(pieces[jnp.bitwise_xor(owner, blk) * visible + (c - owner * visible)])
        blocks.append(
            lax.dot_general(
                jnp.concatenate(picked, axis=1),
                jnp.concatenate([view_ref[r, k] for k in range(nonzero)], axis=1),
                (((1,), (1,)), ((), ())),
                preferred_element_type=F32,
            )
        )
    irradiance = jnp.concatenate(blocks, axis=1)

    patches = cell_ref.shape[0]
    at_low, at_high = cell_masks(cell_ref, depth, width)
    air_cell = air_cell_ref[...]
    temp = temp_ref[...].reshape(1, patches)
    squared = temp * temp
    bands = reflectance_ref.shape[0]
    weight = jnp.zeros((bands, LANES), F32)
    for n in range(bands):
        weight = jnp.where(iota((bands, LANES), 0) == n, weight_ref[n], weight)
    weight = jnp.concatenate([weight] * (patches // LANES), axis=1)
    emission = weight * (emissivity_ref[...].reshape(1, patches) * (squared * squared))
    albedo = reflectance_ref[...].astype(F32)
    radiosity_out[...] = emission + albedo * irradiance
    absorbed = jnp.sum((1.0 - albedo) * irradiance, axis=0, keepdims=True)
    emitted = jnp.sum(emission, axis=0, keepdims=True)
    surface = temp + GAIN * (absorbed - emitted) - COUPLE * (temp - 1.0 - air_cell)
    surface_out[...] = surface
    flux = HEAT * (COUPLE * (surface - 1.0 - air_cell))
    source = sum(
        lax.dot_general(
            jnp.where(at_high, piece.astype(F32), 0.0).astype(BF16),
            at_low,
            (((1,), (1,)), ((), ())),
            preferred_element_type=F32,
        )
        for piece in split(flux, 2)
    )

    for t in range(tiles):
        at = slice(t * LANES, (t + 1) * LANES)
        here = source[t * depth : (t + 1) * depth]
        before = sides[0 if t == 0 else 1, 0] if t in (0, tiles - 1) else ground_ref[:, at]
        ground_out[:, at] = before + here
        for i, x in enumerate((0, 1, depth - 2, depth - 1)):
            source_out[i : i + 1, at] = here[x : x + 1]
    for c in writes:
        c.wait()


def main(
    cols, weight, mine, theirs, reflectance, emissivity, temp, cell, view, air_cell, ground, sides, following
):
    levels, depth = sides.shape[1:3]
    width = ground.shape[1]
    bands, patches = reflectance.shape
    visible = mine.shape[0] // 2 - 6
    return pl.pallas_call(
        main_kernel,
        out_shape=(
            jax.ShapeDtypeStruct((bands, patches), F32),
            jax.ShapeDtypeStruct((1, patches), F32),
            jax.ShapeDtypeStruct(following.shape, F32),
            jax.ShapeDtypeStruct((2, 4, levels, LANES), F32),
            jax.ShapeDtypeStruct((4, width), F32),
            jax.ShapeDtypeStruct((depth, width), F32),
        ),
        in_specs=[pl.BlockSpec(memory_space=SMEM)] * 2 + [WHOLE] * 10 + [PLACE],
        out_specs=(WHOLE, WHOLE, PLACE, WHOLE, WHOLE, WHOLE),
        scratch_shapes=[
            VMEM(sides.shape, F32),
            VMEM((4 * visible, 16, LANES), BF16),
            DMA((2,)),
        ],
        input_output_aliases={12: 2},
        compiler_params=params(20),
        cost_estimate=cost(MAIN_COST),
        name="main",
    )(
        cols,
        weight,
        mine,
        theirs,
        reflectance,
        emissivity,
        temp,
        cell,
        view,
        air_cell,
        ground,
        sides,
        in_hbm(following),
    )


def finish_kernel(
    air_ref,
    edge_ref,
    side_ref,
    source_ref,
    ground_ref,
    radiosity_ref,
    surface_ref,
    near_ref,
    far_ref,
    near_own,
    far_own,
    out_ref,
    radiosity_out,
    surface_out,
    slabs,
    sem,
    value_sem,
):
    del air_ref
    levels, depth, width = out_ref.shape
    parts = levels // 16
    tiles = width // LANES
    district = lax.axis_index("district")
    odd = lax.rem(district, 2)
    has = flag(district > 0), flag(district < lax.axis_size("district") - 1)
    ground = iota((levels, LANES), 0) == 0
    copies = []
    for side in range(2):
        use_near = (odd == 1) if side == 0 else (odd == 0)

        def received(k, i):
            at = [(k * tiles + i) * parts + q for q in range(parts)]
            near, far = (jnp.concatenate([ref[n] for n in at]) for ref in (near_ref, far_ref))
            return jnp.where(use_near, near.astype(F32), far.astype(F32))

        def base(n, i):
            if i in (0, tiles - 1):
                value = side_ref[0 if i == 0 else 1, n]
            else:
                value = edge_ref[n, :, (i - 1) * LANES : i * LANES]
            return value + jnp.where(ground, source_ref[n : n + 1, i * LANES : (i + 1) * LANES], 0.0)

        outer, inner = (0, 1) if side == 0 else (3, 2)
        for i, (c, around) in enumerate(plane_neighbours(functools.partial(received, 0), tiles)):
            at = slice(i * LANES, (i + 1) * LANES)
            own = jnp.where(use_near, near_own[0, :, at], far_own[0, :, at]) * has[side]
            reach = (2.0 * CENTRE) * c + 2.0 * around + received(1, i) + own
            slabs[outer, :, at] = base(outer, i) + SQUARE * reach
            slabs[inner, :, at] = base(inner, i) + SQUARE * c
        for i in (outer, inner):
            x = (0, 1, depth - 2, depth - 1)[i]
            c = pltpu.make_async_copy(slabs.at[i], out_ref.at[:, x, :], sem.at[i])
            c.start()
            copies.append(c)
    small = [
        pltpu.make_async_copy(ground_ref.at[x], out_ref.at[0, x], sem.at[2 + x])
        for x in range(2, depth - 2)
    ]
    small += [
        pltpu.make_async_copy(radiosity_ref, radiosity_out, value_sem.at[0]),
        pltpu.make_async_copy(surface_ref.at[0], surface_out, value_sem.at[1]),
    ]
    for c in small:
        c.start()
    for c in copies + small:
        c.wait()


def finish(air, edge, side, source, ground, radiosity, surface, near, far, near_own, far_own):
    levels, depth, width = air.shape
    return pl.pallas_call(
        finish_kernel,
        out_shape=(
            jax.ShapeDtypeStruct(air.shape, F32),
            jax.ShapeDtypeStruct(radiosity.shape, F32),
            jax.ShapeDtypeStruct(surface.shape[1:], F32),
        ),
        in_specs=[PLACE] + [WHOLE] * 10,
        out_specs=(PLACE,) * 3,
        scratch_shapes=[VMEM((4, levels, width), F32), DMA((depth,)), DMA((2,))],
        input_output_aliases={0: 0},
        compiler_params=params(8),
        name="finish",
    )(in_hbm(air), edge, side, source, ground, radiosity, surface, near, far, near_own, far_own)


def swap(value, axis, pairs):
    return lax.ppermute(value, axis, [p for a, b in pairs for p in ((a, b), (b, a))])


def body(
    view_factor,
    view_cols,
    border_list,
    radiosity,
    reflectance,
    emissivity,
    band_weight,
    surface_temp,
    patch_cell,
    air,
):
    districts, blks = lax.axis_size("district"), lax.axis_size("blk")
    near_pairs = [(i, i + 1) for i in range(0, districts - 1, 2)]
    far_pairs = [(i, i + 1) for i in range(1, districts - 1, 2)]
    near, far_small, own, near_own = pack(border_list, radiosity, air)
    near = swap(near, "district", near_pairs)
    far_small = swap(hold(far_small, own), "district", far_pairs)
    columns = end_columns(air, own)
    once = first(air, columns)
    following, ground, sides, edge, air_cell = second(air, once, patch_cell)
    far, far_own = rows(air, once)
    own = join(own, columns, near, far_small, far)
    far = hold(far, own)
    across = swap(own, "blk", [(i, i ^ 2) for i in range(blks) if i < i ^ 2])
    mine = stack(own, across, far)
    far = swap(far, "district", far_pairs)
    theirs = swap(mine, "blk", [(i, i ^ 1) for i in range(blks) if i < i ^ 1])
    radiosity, surface, air_next, side, source, ground = main(
        view_cols,
        band_weight,
        mine,
        theirs,
        reflectance,
        emissivity,
        surface_temp,
        patch_cell,
        view_factor,
        air_cell,
        ground,
        sides,
        following,
    )
    air_next, radiosity_next, surface_next = finish(
        air_next, edge, side, source, ground, radiosity, surface, near, far, near_own, far_own
    )
    return radiosity_next, surface_next, air_next


def solution(mesh):
    in_specs = (
        P(("district", "blk"), None, None, None),
        P(("district", "blk"), None),
        P(("district", "blk")),
        P(None, ("district", "blk")),
        P(None, ("district", "blk")),
        P(("district", "blk")),
        P(),
        P(("district", "blk")),
        P(("district", "blk")),
        P(None, "district", "blk"),
    )
    out_specs = (P(None, ("district", "blk")), P(("district", "blk")), P(None, "district", "blk"))
    return jax.shard_map(body, mesh=mesh, in_specs=in_specs, out_specs=out_specs, check_vma=False)
```
